512 devices in a mesh: grp: 8 (over x, core), leaf: 64 (over y, z).
Axes of the slice: x: 4, y: 8, z: 8, core: 2. Of those that a mesh axis runs over, the one named last changes fastest.
Arguments:
- points: float32 [16, 1048576], P(None, ('grp', 'leaf')), may hold values from -6 to 6
- rhs: float32 [8, 1048576], P(None, ('grp', 'leaf')), may hold values from -6 to 6
- bases: float32 [8192, 64, 128], P(('grp', 'leaf')), may hold values from -0.5 to 0.5
- up_leaf: float32 [8192, 64, 64], P(('grp', 'leaf')), may hold values from -0.5 to 0.5
- up_cluster: float32 [512, 64, 64], P(('grp', 'leaf')), may hold values from -0.5 to 0.5
- coupling_leaf: float32 [8192, 4, 64, 64], P(('grp', 'leaf')), may hold values from -0.375 to 0.375
- coupling_cluster: float32 [512, 4, 64, 64], P(('grp', 'leaf')), may hold values from -0.09375 to 0.09375
- coupling_group: float32 [8, 8, 64, 64], P('grp'), may hold values from -0.03125 to 0.03125
- near_list: int32 [8192, 8], P(('grp', 'leaf')), may hold values from 0 to 8191, as said below
- near_count: int32 [8192], P(('grp', 'leaf')), may hold values from 1 to 8, as said below
- far_leaf: int32 [8192, 4], P(('grp', 'leaf')), may hold values from 0 to 8191, as said below
- far_cluster: int32 [512, 4], P(('grp', 'leaf')), may hold values from 0 to 511, as said below
Outputs:
- product: float32 [8, 1048576], P(None, ('grp', 'leaf'))
The draws below stay inside these ranges and needn't reach their ends.
Inputs may be any that keep to these rules, and one draw needn't show every extreme that they name: `near_list`: slot 0 of row l is l itself; the other slots hold distinct leaves other than l, owned by the device of l or by the device just before or just after it, devices being ordered by grp then leaf, device d owning leaves d * 16 to d * 16 + 15. Only the first near_count[l] slots of row l of near_list are used. `far_leaf`: the entries of row l lie in the group of l, on distinct devices other than the device of l; taken over the 16 leaves of one device, at most 2 entries lie on any one device, and some device receives exactly that many. `far_cluster`: every entry of row c lies in the group of c, two or more places away from c within that group.
All inputs are finite; a program needn't handle non-finite values.
Results may differ from the reference program's by a relative error of at most 0.0003.
Values sent between devices are 32-bit elements; how exact they have to be, the bound alone decides.
A program may use at most 64 MiB of HBM per device.

```python
import jax
import jax.numpy as jnp
from jax import lax

LEAF = 128
RANK = 64
DIM = 16
NRHS = 8
LEAF_DEV = 16
NEAR = 8
FAR2 = 4
FAR1 = 4
CLUS_GRP = 64
NGRP = 8
CLUSTERS = 512
LEAVES = 8192
NPTS = 1048576


def draw_near_list(key, part):
    leaf_ids = jnp.arange(LEAVES, dtype=jnp.int32)
    device = leaf_ids // LEAF_DEV
    offsets = jnp.arange(3 * LEAF_DEV, dtype=jnp.int32)
    cand = device[:, None] * LEAF_DEV - LEAF_DEV + offsets[None, :]
    valid = (cand >= 0) & (cand < LEAVES) & (cand != leaf_ids[:, None])
    scores = jax.random.randint(key, (LEAVES, 3 * LEAF_DEV), 0, 1 << 20, dtype=jnp.int32) * (4 * LEAF_DEV) + offsets[None, :]
    scores = jnp.where(valid, scores, (1 << 30) + offsets[None, :])
    order = jnp.argsort(scores, axis=1, stable=True)
    chosen = jnp.take_along_axis(cand, order[:, :NEAR - 1], axis=1)
    return jnp.concatenate([leaf_ids[:, None], chosen], axis=1).astype(jnp.int32)


def draw_near_count(key, part):
    caps = jax.random.randint(jax.random.fold_in(key, 1), (LEAVES // LEAF_DEV,), 2, NEAR + 1, dtype=jnp.int32)
    per_leaf = jnp.repeat(caps, LEAF_DEV, total_repeat_length=LEAVES)
    counts = jax.random.randint(jax.random.fold_in(key, 2), (LEAVES,), 1, per_leaf + 1, dtype=jnp.int32)
    counts = counts.at[0].set(NEAR).at[LEAVES - 1].set(1)
    return counts.astype(jnp.int32)


def draw_far_leaf(key, part):
    leaf_ids = jnp.arange(LEAVES, dtype=jnp.int32)
    device = leaf_ids // LEAF_DEV
    local_j = leaf_ids % LEAF_DEV
    group = device // CLUS_GRP
    place = device % CLUS_GRP
    span = CLUS_GRP - 1
    shifts = jax.random.randint(jax.random.fold_in(key, 1), (CLUSTERS,), 0, span, dtype=jnp.int32)
    shift = jnp.take(shifts, device)
    slots = jnp.arange(FAR2, dtype=jnp.int32)
    turn = (local_j[:, None] * FAR2 + slots[None, :] + shift[:, None]) % span
    target = group[:, None] * CLUS_GRP + (place[:, None] + 1 + turn) % CLUS_GRP
    inner = jax.random.randint(jax.random.fold_in(key, 2), (LEAVES, FAR2), 0, LEAF_DEV, dtype=jnp.int32)
    return (target * LEAF_DEV + inner).astype(jnp.int32)


def draw_far_cluster(key, part):
    cluster_ids = jnp.arange(CLUSTERS, dtype=jnp.int32)
    group = cluster_ids // CLUS_GRP
    offsets = jnp.arange(CLUS_GRP, dtype=jnp.int32)
    cand = group[:, None] * CLUS_GRP + offsets[None, :]
    close = jnp.abs(cand - cluster_ids[:, None]) <= 1
    scores = jax.random.randint(key, (CLUSTERS, CLUS_GRP), 0, 1 << 16, dtype=jnp.int32) * CLUS_GRP + offsets[None, :]
    scores = jnp.where(close, (1 << 30) + offsets[None, :], scores)
    order = jnp.argsort(scores, axis=1, stable=True)
    chosen = jnp.take_along_axis(cand, order[:, :FAR1], axis=1)
    chosen = chosen.at[CLUS_GRP - 1, 0].set(0).at[CLUSTERS - CLUS_GRP, 0].set(CLUSTERS - 1)
    return chosen.astype(jnp.int32)


def level_of(key, shape, shards, least, top_value):
    loudness = 1.0
    for axis_at, blocks in shards:
        heights = jax.random.uniform(jax.random.fold_in(jax.random.fold_in(key, 6), axis_at), (blocks,), jnp.float32, least / len(shards), top_value / len(shards))
        loudness = loudness * jnp.repeat(jnp.exp(heights), shape[axis_at] // blocks).reshape((-1,) + (1,) * (len(shape) - 1 - axis_at))
    return loudness


def bell_draw(own_key, dims, width, reach, split=(), kind=jnp.bfloat16):
    entries = width * jax.random.normal(own_key, dims, jnp.float32)
    if split:
        entries = entries * level_of(own_key, dims, split, -0.22, 0.18)
    return jnp.clip(entries, -reach, reach).astype(kind)


def setup_inputs(seed: int = 0) -> dict:
    splits = jax.random.split(jax.random.key(seed), 13)
    points = bell_draw(splits[0], (DIM, NPTS), 1.0, 6.0, ((1, 512),), jnp.float32)
    rhs = bell_draw(splits[1], (NRHS, NPTS), 1.0, 6.0, ((1, 512),), jnp.float32)
    bases = bell_draw(splits[2], (LEAVES, RANK, LEAF), LEAF ** -0.5, 0.5, ((0, 512),), jnp.float32)
    up_leaf = bell_draw(splits[3], (LEAVES, RANK, RANK), (2 * RANK) ** -0.5, 0.5, ((0, 512),), jnp.float32)
    up_cluster = bell_draw(splits[4], (CLUSTERS, RANK, RANK), (2 * RANK) ** -0.5, 0.5, ((0, 512),), jnp.float32)
    coupling_leaf = bell_draw(splits[5], (LEAVES, FAR2, RANK, RANK), (RANK * FAR2) ** -0.5, 0.375, ((0, 512),), jnp.float32)
    coupling_cluster = bell_draw(splits[6], (CLUSTERS, FAR1, RANK, RANK), (RANK * FAR1 * LEAF_DEV) ** -0.5, 0.09375, ((0, 512),), jnp.float32)
    coupling_group = bell_draw(splits[7], (NGRP, NGRP, RANK, RANK), (RANK * NGRP * CLUS_GRP) ** -0.5, 0.03125, ((0, 8),), jnp.float32)
    near_list = draw_near_list(jax.random.fold_in(splits[12], 71), 0)
    near_count = draw_near_count(jax.random.fold_in(splits[12], 71), 0)
    far_leaf = draw_far_leaf(jax.random.fold_in(splits[12], 71), 0)
    far_cluster = draw_far_cluster(jax.random.fold_in(splits[12], 71), 0)
    return {"points": points, "rhs": rhs, "bases": bases, "up_leaf": up_leaf, "up_cluster": up_cluster, "coupling_leaf": coupling_leaf, "coupling_cluster": coupling_cluster, "coupling_group": coupling_group, "near_list": near_list, "near_count": near_count, "far_leaf": far_leaf, "far_cluster": far_cluster}


HIGHEST = lax.Precision.HIGHEST
RATE = 0.8660254037844386

def matern(left, right):
    cross = jnp.einsum('dbp,dbkq->bkpq', left, right, precision=HIGHEST)
    left_sq = lax.optimization_barrier(jnp.sum(left * left, axis=0))
    right_sq = lax.optimization_barrier(jnp.sum(right * right, axis=0))
    gap = left_sq[:, None, :, None] + right_sq[:, :, None, :] - 2.0 * cross
    scaled = RATE * jnp.sqrt(jnp.maximum(gap, 0.0))
    return (1.0 + scaled) * jnp.exp(-scaled)

def near_field(points, rhs, near_list, near_count):
    leaves = near_list.shape[0]
    block = LEAF_DEV
    nblocks = leaves // block
    coords = points.reshape(DIM, leaves, LEAF)
    values = rhs.reshape(NRHS, leaves, LEAF)

    def one_block(item):
        own, index, count = item
        left = jnp.take(coords, own, axis=1)
        right = jnp.take(coords, index.reshape(-1), axis=1).reshape(DIM, block, NEAR, LEAF)
        weights = jnp.take(values, index.reshape(-1), axis=1).reshape(NRHS, block, NEAR, LEAF)
        tile = matern(left, right)
        live = (jnp.arange(NEAR)[None, :] < count[:, None]).astype(jnp.float32)
        return jnp.einsum('bkpq,sbkq->sbp', tile * live[:, :, None, None], weights, precision=HIGHEST)
    owners = jnp.arange(leaves, dtype=jnp.int32).reshape(nblocks, block)
    result = lax.map(one_block, (owners, near_list.reshape(nblocks, block, NEAR), near_count.reshape(nblocks, block)))
    return result.transpose(1, 0, 2, 3).reshape(NRHS, leaves * LEAF)

def reference(points, rhs, bases, up_leaf, up_cluster, coupling_leaf, coupling_cluster, coupling_group, near_list, near_count, far_leaf, far_cluster):
    leaves = bases.shape[0]
    clusters = up_cluster.shape[0]
    groups = coupling_group.shape[0]
    rhs_leaves = rhs.reshape(NRHS, leaves, LEAF)
    coef = jnp.einsum('lrp,slp->slr', bases, rhs_leaves, precision=HIGHEST)
    leaf_blocks = up_leaf.reshape(clusters, LEAF_DEV, RANK, RANK)
    cluster_coef = jnp.einsum('scjr,cjrq->scq', coef.reshape(NRHS, clusters, LEAF_DEV, RANK), leaf_blocks, precision=HIGHEST)
    terms = jnp.einsum('scr,crq->scq', cluster_coef, up_cluster, precision=HIGHEST)
    group_coef = terms.reshape(NRHS, groups, clusters // groups, RANK).sum(axis=2)
    others = (jnp.arange(groups)[:, None] != jnp.arange(groups)[None, :]).astype(jnp.float32)
    field_group = jnp.einsum('ghrq,shq->sgr', coupling_group * others[:, :, None, None], group_coef, precision=HIGHEST)
    picked_cluster = jnp.take(cluster_coef, far_cluster, axis=1)
    field_cluster = jnp.einsum('ckrq,sckq->scr', coupling_cluster, picked_cluster, precision=HIGHEST)
    spread_group = jnp.repeat(field_group, clusters // groups, axis=1)
    field_cluster = field_cluster + jnp.einsum('crq,scq->scr', up_cluster, spread_group, precision=HIGHEST)
    picked_leaf = jnp.take(coef, far_leaf, axis=1)
    field = jnp.einsum('lkrq,slkq->slr', coupling_leaf, picked_leaf, precision=HIGHEST)
    down = jnp.einsum('cjrq,scq->scjr', leaf_blocks, field_cluster, precision=HIGHEST)
    field = field + down.reshape(NRHS, leaves, RANK)
    far_out = jnp.einsum('lrp,slr->slp', bases, field, precision=HIGHEST).reshape(NRHS, leaves * LEAF)
    return far_out + near_field(points, rhs, near_list, near_count)
```

```python
import functools

import jax
import jax.numpy as jnp
from jax import lax
from jax.experimental import pallas as pl
from jax.experimental.pallas import tpu as pltpu
from jax.sharding import PartitionSpec as P

F32, BF16, I32 = jnp.float32, jnp.bfloat16, jnp.int32
MESH = pl.DeviceIdType.MESH


def iota(shape, dim):
    return lax.broadcasted_iota(I32, shape, dim)


def rounded(x):
    return x.astype(BF16).astype(F32)


def halves(x):
    high = x.astype(BF16)
    return high, (x - high.astype(F32)).astype(BF16)


def stack16(x):
    high = rounded(x)
    return jnp.concatenate([high, x - high], axis=0).astype(BF16)


def fold(x):
    return x[:8] + x[8:]


def nn(a, b):
    return lax.dot_general(a, b, (((1,), (0,)), ((), ())), preferred_element_type=F32)


def nt(a, b):
    return lax.dot_general(a, b, (((1,), (1,)), ((), ())), preferred_element_type=F32)


def split_dot(dot, x16, w):
    high, low = halves(w)
    return fold(dot(x16, high) + dot(x16, low))


def thirds(x):
    high = rounded(x)
    rest = x - high
    mid = rounded(rest)
    return high, mid, rest - mid


def norm_rows(norm, first):
    high, mid, low = thirds(norm)
    row = iota((32, norm.shape[1]), 0)
    at = row - first
    split = jnp.where(at == 0, high, jnp.where(at == 1, mid, jnp.where(at == 2, low, 0.0)))
    return jnp.where((row < 6) & ((at < 0) | (at > 2)), 1.0, split)


def kernel(
    side,
    n_grp,
    near_s,
    count_s,
    farc_s,
    pts_h,
    rhs_h,
    bases_h,
    upl_h,
    upc_h,
    cpl_h,
    cpc_h,
    cpg_h,
    farl_h,
    out_ref,
    st,
    bases_v,
    upl_v,
    upc_v,
    cpl_v,
    cpc_v,
    cpg_v,
    farl_v,
    bhi,
    blo,
    uhi,
    ulo,
    chi,
    clo,
    left_t,
    right,
    weight,
    coef2,
    near_out,
    down,
    tab_v,
    tab_s,
    ridx,
    reqz,
    reqy,
    ctz,
    cty,
    gcb,
    rows_out,
    rows_in,
    load_sem,
    tab_sem,
    st_send,
    st_recv,
    x_send,
    x_recv,
):
    n_leaf = side * side
    many = n_grp * n_leaf
    leaf_dev = bases_v.shape[0]
    grp, leaf = lax.axis_index("grp"), lax.axis_index("leaf")
    y, z = lax.div(leaf, side), lax.rem(leaf, side)
    dev = grp * n_leaf + leaf

    def at_dev(d):
        return lax.div(d, n_leaf), lax.rem(d, n_leaf)

    after, before = at_dev(lax.rem(dev + 1, many)), at_dev(lax.rem(dev + many - 1, many))

    barrier = pltpu.get_barrier_semaphore()

    def greet(who):
        pl.semaphore_signal(barrier, inc=1, device_id=who, device_id_type=MESH)

    greet(after)
    greet(before)

    def greet_leaf(j, c):
        greet((grp, lax.rem(leaf + j, n_leaf)))
        return c

    def greet_grp(j, c):
        greet((lax.rem(grp + j, n_grp), leaf))
        return c

    lax.fori_loop(1, n_leaf, greet_leaf, 0)
    lax.fori_loop(1, n_grp, greet_grp, 0)

    loads = {}
    plan = (
        ("farl", farl_h, farl_v),
        ("pts", pts_h, st.at[1, pl.ds(0, 16)]),
        ("rhs", rhs_h, st.at[1, pl.ds(16, 8)]),
        ("bases", bases_h, bases_v),
        ("upl", upl_h, upl_v),
        ("upc", upc_h, upc_v),
        ("cpl", cpl_h, cpl_v),
        ("cpc", cpc_h, cpc_v),
        ("cpg", cpg_h, cpg_v),
    )
    for i, (name, src, dst) in enumerate(plan):
        loads[name] = pltpu.make_async_copy(src, dst, load_sem.at[i])
        loads[name].start()

    def exchange(buf, at, peer, count, i):
        def go(j, c):
            pltpu.make_async_remote_copy(
                src_ref=buf.at[at],
                dst_ref=buf.at[at],
                send_sem=x_send.at[i],
                recv_sem=x_recv.at[i],
                device_id=peer(j),
                device_id_type=MESH,
            ).start()
            return c

        lax.fori_loop(1, count, go, 0)

    def arrived(ref, sem):
        pltpu.make_async_copy(ref, ref, sem).wait()

    def z_peer(j):
        return grp, y * side + lax.rem(z + j, side)

    def y_peer(j):
        return grp, lax.rem(y + j, side) * side + z

    def g_peer(j):
        return lax.rem(grp + j, n_grp), leaf

    loads["farl"].wait()
    far = farl_v[...]
    far_two = far.shape[1]
    lane, sub = iota((leaf_dev, 128), 1), iota((leaf_dev, 128), 0)
    wide = jnp.zeros((leaf_dev, 128), I32)
    for k in range(far_two):
        wide = jnp.where(lane == sub + leaf_dev * k, far[:, k : k + 1], wide)
    asks = leaf_dev * far_two
    row = jnp.sum(wide, axis=0, keepdims=True)
    row = jnp.where(iota((1, 128), 1) < asks, row, -1)
    reqz[z] = jnp.broadcast_to(row, (8, 128))
    owner = row >> 4
    lane_f, sub_f = iota((asks, 128), 1), iota((asks, 128), 0)
    spread = jnp.broadcast_to(owner.astype(F32), (asks, 128))
    column = jnp.sum(jnp.where(lane_f == sub_f, spread, 0.0), axis=1, keepdims=True)
    again = jnp.where((sub_f < lane_f) & (spread == column), 1.0, 0.0)
    again = jnp.max(again, axis=0, keepdims=True).astype(I32)
    place = ((leaf - (owner - grp * n_leaf)) & (n_leaf - 1)) - 1
    tab_v[...] = place * 2 + again
    tab_copy = pltpu.make_async_copy(tab_v, tab_s, tab_sem)
    tab_copy.start()

    loads["pts"].wait()
    loads["rhs"].wait()
    pl.semaphore_wait(barrier, n_leaf + n_grp)

    exchange(reqz, z, z_peer, side, 0)
    sides = []
    for i, (who, slot) in enumerate(((after, 0), (before, 2))):
        copy = pltpu.make_async_remote_copy(
            src_ref=st.at[1],
            dst_ref=st.at[slot],
            send_sem=st_send.at[i],
            recv_sem=st_recv.at[i],
            device_id=who,
            device_id_type=MESH,
        )
        copy.start()
        sides.append(copy)

    loads["bases"].wait()
    loads["upl"].wait()
    cc = jnp.zeros((16, 64), F32)
    for l in range(leaf_dev):
        x16 = stack16(st[1, 16:24, l * 128 : (l + 1) * 128])
        high, low = halves(bases_v[l])
        bhi[l], blo[l] = high, low
        two_high = jnp.concatenate([high, high], axis=0)
        two_low = jnp.concatenate([low, low], axis=0)
        c2 = fold(nt(x16, two_high) + nt(x16, two_low))
        coef2[l] = c2
        high, low = halves(upl_v[l])
        uhi[l], ulo[l] = high, low
        cc = cc + nn(stack16(c2), jnp.concatenate([high, low], axis=0))
    cc = fold(cc)
    loads["upc"].wait()
    term = split_dot(nn, stack16(cc), upc_v[0])
    ctz[z] = jnp.concatenate([cc, term], axis=1)
    exchange(ctz, z, z_peer, side, 1)

    arrived(reqz.at[pl.ds(0, side - 1)], x_recv.at[0])
    row8 = iota((8, 128), 0)
    tile = reqz[0]
    for i in range(1, side):
        tile = jnp.where(row8 == i, reqz[i], tile)
    reqy[y] = tile
    exchange(reqy, y, y_peer, side, 2)

    def features(block, m):
        a = st[block, 0:16, pl.ds(pl.multiple_of(m * 128, 128), 128)]
        return a, 0.75 * jnp.sum(a * a, axis=0, keepdims=True)

    def put_right(block, m, c):
        b, norm = features(block, m)
        high, mid, low = thirds(b)
        parts = [high, mid, high, mid, low, high, norm_rows(norm, 0)]
        right[block * leaf_dev + m] = jnp.concatenate(parts, axis=0).astype(BF16)
        x = st[block, 16:24, pl.ds(pl.multiple_of(m * 128, 128), 128)]
        top = rounded(x)
        first = jnp.concatenate([top, x - top], axis=0)
        second = jnp.concatenate([top, jnp.zeros_like(top)], axis=0)
        weight[block * leaf_dev + m] = jnp.concatenate([first, second], axis=1).astype(BF16)
        return c

    def put_left(l, c):
        a, norm = features(1, l)
        high, mid, low = thirds(-1.5 * a)
        parts = [high, high, mid, mid, high, low, norm_rows(norm, 3)]
        left_t[l] = jnp.concatenate(parts, axis=0).T.astype(BF16)
        return c

    lax.fori_loop(0, leaf_dev, put_left, 0)
    lax.fori_loop(0, leaf_dev, functools.partial(put_right, 1), 0)

    arrived(ctz.at[pl.ds(0, side - 1)], x_recv.at[1])
    low_lanes = iota((8, 128), 1) < 64
    total = ctz[0]
    for i in range(1, side):
        total = total + ctz[i]
    for i in range(side // 2):
        cty[y, i] = jnp.where(low_lanes, ctz[2 * i], pltpu.roll(ctz[2 * i + 1], 64, 1))
    cty[y, side // 2] = total
    exchange(cty, y, y_peer, side, 3)

    arrived(reqy.at[pl.ds(0, side - 1)], x_recv.at[2])
    lane8 = iota((8, 128), 1)
    for i in range(side):
        asked = reqy[i]
        mine = (asked >> 4) == dev
        code = (lane8 * 16 + (asked & 15)).astype(F32)
        first = jnp.min(jnp.where(mine, code, 4096.0), axis=1, keepdims=True)
        last = jnp.max(jnp.where(mine, code, 0.0), axis=1, keepdims=True)
        ridx[i * 8 : (i + 1) * 8] = jnp.where(low_lanes, first, last).astype(I32) & 15

    def send_row(j, c):
        who = lax.rem(leaf + j, n_leaf)
        index = jnp.broadcast_to(ridx[pl.ds(who, 1), :], (8, 128))
        picked = coef2[0]
        for l in range(1, leaf_dev):
            picked = jnp.where(index == l, coef2[l], picked)
        rows_out[j - 1] = picked
        pltpu.make_async_remote_copy(
            src_ref=rows_out.at[j - 1],
            dst_ref=rows_in.at[j - 1],
            send_sem=x_send.at[5],
            recv_sem=x_recv.at[5],
            device_id=(grp, who),
            device_id_type=MESH,
        ).start()
        return c

    lax.fori_loop(1, n_leaf, send_row, 0)

    loads["cpl"].wait()

    def put_coupling(l, c):
        parts = [cpl_v[l, k] for k in range(far_two)]
        high, low = halves(jnp.concatenate(parts, axis=1))
        chi[l], clo[l] = high, low
        return c

    lax.fori_loop(0, leaf_dev, put_coupling, 0)

    arrived(cty.at[pl.ds(0, side - 1)], x_recv.at[3])
    total = cty[0, side // 2]
    for i in range(1, side):
        total = total + cty[i, side // 2]
    gcb[grp] = total
    exchange(gcb, grp, g_peer, n_grp, 4)

    for copy in sides:
        copy.wait_recv()
    lax.fori_loop(0, leaf_dev, functools.partial(put_right, 0), 0)
    lax.fori_loop(0, leaf_dev, functools.partial(put_right, 2), 0)
    slots = near_s.shape[1]
    base = (dev - 1) * leaf_dev

    def near_leaf(l, c):
        lhs = left_t[l]
        count = count_s[l]
        acc = jnp.zeros((16, 128), F32)
        for k in range(slots):
            m = jnp.clip(near_s[l, k] - base, 0, 3 * leaf_dev - 1)
            gap = jnp.maximum(nn(lhs, right[m]), 1e-30)
            u = gap * lax.rsqrt(gap)
            value = (1.0 + u) * jnp.exp(-u)
            high = value.astype(BF16)
            low = (value - high.astype(F32)).astype(BF16)
            live = jnp.where(k < count, 1.0, 0.0).astype(F32)
            part = nt(weight[m], jnp.concatenate([high, low], axis=1))
            acc = acc + live * part
        near_out[l] = fold(acc)
        return c

    lax.fori_loop(0, leaf_dev, near_leaf, 0)

    arrived(gcb.at[pl.ds(0, n_grp - 1)], x_recv.at[4])
    loads["cpc"].wait()
    loads["cpg"].wait()
    field_group = jnp.zeros((8, 64), F32)
    for h in range(n_grp):
        other = jnp.where(grp == h, 0.0, 1.0).astype(F32)
        gc = gcb[h][:, 64:] * other
        field_group = field_group + split_dot(nt, stack16(gc), cpg_v[0, h])
    field_cluster = split_dot(nt, stack16(field_group), upc_v[0])
    for k in range(cpc_v.shape[1]):
        f = jnp.clip(farc_s[0, k] - grp * n_leaf, 0, n_leaf - 1)
        fy, fz = lax.div(f, side), lax.rem(f, side)
        pair = cty[fy, lax.div(fz, 2)]
        flag = jnp.full((8, 128), lax.rem(fz, 2), I32)
        one = jnp.where(flag == 1, pltpu.roll(pair, 64, 1), pair)[:, :64]
        field_cluster = field_cluster + split_dot(nt, stack16(one), cpc_v[0, k])
    fc16 = stack16(field_cluster)
    for l in range(leaf_dev):
        down[l] = fold(nt(fc16, uhi[l]) + nt(fc16, ulo[l]))

    arrived(rows_in, x_recv.at[5])
    tab_copy.wait()
    for l in range(leaf_dev):
        chunks = []
        for pair in range(far_two // 2):
            both = []
            for half in range(2):
                t = tab_s[0, (2 * pair + half) * leaf_dev + l]
                got = rows_in[jnp.clip(t >> 1, 0, n_leaf - 2)]
                flag = jnp.full((8, 128), t & 1, I32)
                both.append(jnp.where(flag == half, got, pltpu.roll(got, 64, 1)))
            chunks.append(jnp.where(low_lanes, both[0], both[1]))
        x16 = stack16(jnp.concatenate(chunks, axis=1))
        field = fold(nt(x16, chi[l]) + nt(x16, clo[l])) + down[l]
        f16 = stack16(field)
        out_ref[:, l * 128 : (l + 1) * 128] = fold(nn(f16, bhi[l]) + nn(f16, blo[l])) + near_out[l]

    for copy in sides:
        copy.wait_send()
    for i, buf, n in ((0, reqz, side), (1, ctz, side), (2, reqy, side), (3, cty, side), (4, gcb, n_grp)):
        arrived(buf.at[pl.ds(0, n - 1)], x_send.at[i])
    arrived(rows_out, x_send.at[5])


def per_device(
    points,
    rhs,
    bases,
    up_leaf,
    up_cluster,
    coupling_leaf,
    coupling_cluster,
    coupling_group,
    near_list,
    near_count,
    far_leaf,
    far_cluster,
):
    n_leaf, n_grp = lax.axis_size("leaf"), lax.axis_size("grp")
    side = round(n_leaf**0.5)
    leaf_dev, rank, width = bases.shape
    nrhs = rhs.shape[0]
    far_two = far_leaf.shape[1]
    anywhere = pl.BlockSpec(memory_space=pl.ANY)
    scalars = pl.BlockSpec(memory_space=pltpu.SMEM)
    vmem = pltpu.VMEM
    return pl.pallas_call(
        functools.partial(kernel, side, n_grp),
        out_shape=jax.ShapeDtypeStruct(rhs.shape, F32),
        in_specs=[scalars] * 3 + [anywhere] * 9,
        out_specs=pl.BlockSpec(memory_space=vmem),
        scratch_shapes=[
            vmem((3, 24, points.shape[1]), F32),
            vmem(bases.shape, F32),
            vmem(up_leaf.shape, F32),
            vmem(up_cluster.shape, F32),
            vmem(coupling_leaf.shape, F32),
            vmem(coupling_cluster.shape, F32),
            vmem(coupling_group.shape, F32),
            vmem(far_leaf.shape, I32),
            vmem(bases.shape, BF16),
            vmem(bases.shape, BF16),
            vmem(up_leaf.shape, BF16),
            vmem(up_leaf.shape, BF16),
            vmem((leaf_dev, rank, far_two * rank), BF16),
            vmem((leaf_dev, rank, far_two * rank), BF16),
            vmem((leaf_dev, width, 128), BF16),
            vmem((3 * leaf_dev, 128, width), BF16),
            vmem((3 * leaf_dev, 16, 2 * width), BF16),
            vmem((leaf_dev, nrhs, 128), F32),
            vmem((leaf_dev, nrhs, width), F32),
            vmem((leaf_dev, nrhs, rank), F32),
            vmem((1, 128), I32),
            pltpu.SMEM((1, 128), I32),
            vmem((n_leaf, 128), I32),
            vmem((side, 8, 128), I32),
            vmem((side, 8, 128), I32),
            vmem((side, 8, 128), F32),
            vmem((side, side // 2 + 1, 8, 128), F32),
            vmem((n_grp, 8, 128), F32),
            vmem((n_leaf - 1, 8, 128), F32),
            vmem((n_leaf - 1, 8, 128), F32),
            pltpu.SemaphoreType.DMA((9,)),
            pltpu.SemaphoreType.DMA,
            pltpu.SemaphoreType.DMA((2,)),
            pltpu.SemaphoreType.DMA((2,)),
            pltpu.SemaphoreType.DMA((6,)),
            pltpu.SemaphoreType.DMA((6,)),
        ],
        compiler_params=pltpu.CompilerParams(
            collective_id=0, has_side_effects=True, vmem_limit_bytes=32 * 1024 * 1024
        ),
    )(
        near_list,
        near_count,
        far_cluster,
        points,
        rhs,
        bases,
        up_leaf,
        up_cluster,
        coupling_leaf,
        coupling_cluster,
        coupling_group,
        far_leaf,
    )


def solution(mesh):
    placed = (
        P(None, ("grp", "leaf")),
        P(None, ("grp", "leaf")),
        P(("grp", "leaf"), None, None),
        P(("grp", "leaf"), None, None),
        P(("grp", "leaf"), None, None),
        P(("grp", "leaf"), None, None, None),
        P(("grp", "leaf"), None, None, None),
        P("grp", None, None, None),
        P(("grp", "leaf"), None),
        P(("grp", "leaf")),
        P(("grp", "leaf"), None),
        P(("grp", "leaf"), None),
    )
    return jax.shard_map(
        per_device, mesh=mesh, in_specs=placed, out_specs=P(None, ("grp", "leaf")), check_vma=False
    )
```

```python
import functools

import jax
import jax.numpy as jnp
from jax import lax
from jax.experimental import pallas as pl
from jax.experimental.pallas import tpu as pltpu
from jax.sharding import PartitionSpec as P

F32, BF16, I32 = jnp.float32, jnp.bfloat16, jnp.int32
MESH = pl.DeviceIdType.MESH


def loop(start, stop, step, body):
    def some(i, c):
        for j in range(step):
            body(start + i * step + j)
        return c

    lax.fori_loop(0, (stop - start) // step, some, 0)


def iota(shape, dim):
    return lax.broadcasted_iota(I32, shape, dim)


def rounded(x):
    return x.astype(BF16).astype(F32)


def halves(x):
    high = x.astype(BF16)
    return high, (x - high.astype(F32)).astype(BF16)


def stack16(x):
    high = rounded(x)
    return jnp.concatenate([high, x - high], axis=0).astype(BF16)


def fold(x):
    return x[:8] + x[8:]


def nn(a, b):
    return lax.dot_general(a, b, (((1,), (0,)), ((), ())), preferred_element_type=F32)


def nt(a, b):
    return lax.dot_general(a, b, (((1,), (1,)), ((), ())), preferred_element_type=F32)


def split_dot(dot, x16, w):
    high, low = halves(w)
    return fold(dot(x16, high) + dot(x16, low))


def thirds(x):
    high = rounded(x)
    rest = x - high
    mid = rounded(rest)
    return high, mid, rest - mid


def norm_rows(norm, first):
    high, mid, low = thirds(norm)
    row = iota((32, norm.shape[1]), 0)
    at = row - first
    split = jnp.where(at == 0, high, jnp.where(at == 1, mid, jnp.where(at == 2, low, 0.0)))
    return jnp.where((row < 6) & ((at < 0) | (at > 2)), 1.0, split)


def kernel(
    side,
    n_grp,
    near_s,
    count_s,
    farc_s,
    pts_h,
    rhs_h,
    bases_h,
    upl_h,
    upc_h,
    cpl_h,
    cpc_h,
    cpg_h,
    farl_h,
    out_ref,
    st,
    bases_v,
    upl_v,
    upc_v,
    cpl_v,
    cpc_v,
    cpg_v,
    farl_v,
    bhi,
    blo,
    uhi,
    ulo,
    chi,
    clo,
    left,
    right,
    weight,
    coef2,
    near_out,
    down,
    tab_v,
    tab_s,
    ridx,
    reqz,
    reqy,
    ctz,
    cty,
    gcb,
    rows_out,
    rows_in,
    load_sem,
    tab_sem,
    st_send,
    st_recv,
    x_send,
    x_recv,
):
    n_leaf = side * side
    many = n_grp * n_leaf
    leaf_dev = bases_v.shape[0]
    grp, leaf = lax.axis_index("grp"), lax.axis_index("leaf")
    y, z = lax.div(leaf, side), lax.rem(leaf, side)
    dev = grp * n_leaf + leaf

    def at_dev(d):
        return lax.div(d, n_leaf), lax.rem(d, n_leaf)

    after, before = at_dev(lax.rem(dev + 1, many)), at_dev(lax.rem(dev + many - 1, many))

    loads = {}
    plan = (
        ("farl", farl_h, farl_v),
        ("pts", pts_h, st.at[1, pl.ds(0, 16)]),
        ("rhs", rhs_h, st.at[1, pl.ds(16, 8)]),
        ("bases", bases_h, bases_v),
        ("upl", upl_h, upl_v),
        ("upc", upc_h, upc_v),
        ("cpl", cpl_h, cpl_v),
        ("cpc", cpc_h, cpc_v),
        ("cpg", cpg_h, cpg_v),
    )
    for i, (name, src, dst) in enumerate(plan):
        loads[name] = pltpu.make_async_copy(src, dst, load_sem.at[i])
        loads[name].start()

    barrier = pltpu.get_barrier_semaphore()

    def greet(who):
        pl.semaphore_signal(barrier, inc=1, device_id=who, device_id_type=MESH)

    greet(after)
    greet(before)

    loop(1, n_leaf, 7, lambda j: greet((grp, lax.rem(leaf + j, n_leaf))))
    loop(1, n_grp, 7, lambda j: greet((lax.rem(grp + j, n_grp), leaf)))

    def exchange(buf, at, peer, count, i):
        def go(j):
            pltpu.make_async_remote_copy(
                src_ref=buf.at[at],
                dst_ref=buf.at[at],
                send_sem=x_send.at[i],
                recv_sem=x_recv.at[i],
                device_id=peer(j),
                device_id_type=MESH,
            ).start()

        loop(1, count, 7, go)

    def arrived(ref, sem):
        pltpu.make_async_copy(ref, ref, sem).wait()

    def z_peer(j):
        return grp, y * side + lax.rem(z + j, side)

    def y_peer(j):
        return grp, lax.rem(y + j, side) * side + z

    def g_peer(j):
        return lax.rem(grp + j, n_grp), leaf

    loads["farl"].wait()
    far = farl_v[...]
    far_two = far.shape[0]
    asks = leaf_dev * far_two
    parts = [far[k : k + 1] for k in range(far_two)]
    row = jnp.concatenate([*parts, jnp.full((1, 128 - asks), -1, I32)], axis=1)
    reqz[z] = jnp.broadcast_to(row, (8, 128))
    owner = row >> 4
    lane_f, sub_f = iota((asks, 128), 1), iota((asks, 128), 0)
    spread = jnp.broadcast_to(owner.astype(F32), (asks, 128))
    column = jnp.sum(jnp.where(lane_f == sub_f, spread, 0.0), axis=1, keepdims=True)
    again = jnp.where((sub_f < lane_f) & (spread == column), 1.0, 0.0)
    again = jnp.max(again, axis=0, keepdims=True).astype(I32)
    place = ((leaf - (owner - grp * n_leaf)) & (n_leaf - 1)) - 1
    tab_v[...] = place * 2 + again
    tab_copy = pltpu.make_async_copy(tab_v, tab_s, tab_sem)
    tab_copy.start()

    loads["pts"].wait()
    loads["rhs"].wait()
    pl.semaphore_wait(barrier, n_leaf + n_grp)

    exchange(reqz, z, z_peer, side, 0)
    sides = []
    for i, (who, slot) in enumerate(((after, 0), (before, 2))):
        copy = pltpu.make_async_remote_copy(
            src_ref=st.at[1],
            dst_ref=st.at[slot],
            send_sem=st_send.at[i],
            recv_sem=st_recv.at[i],
            device_id=who,
            device_id_type=MESH,
        )
        copy.start()
        sides.append(copy)

    loads["bases"].wait()
    loads["upl"].wait()
    cc = jnp.zeros((16, 64), F32)
    for l in range(leaf_dev):
        x16 = stack16(st[1, 16:24, l * 128 : (l + 1) * 128])
        high, low = halves(bases_v[l])
        bhi[l], blo[l] = high, low
        two_high = jnp.concatenate([high, high], axis=0)
        two_low = jnp.concatenate([low, low], axis=0)
        c2 = fold(nt(x16, two_high) + nt(x16, two_low))
        coef2[l] = c2
        high, low = halves(upl_v[l])
        uhi[l], ulo[l] = high, low
        cc = cc + nn(stack16(c2), jnp.concatenate([high, low], axis=0))
    cc = fold(cc)
    loads["upc"].wait()
    term = split_dot(nn, stack16(cc), upc_v[0])
    ctz[z] = jnp.concatenate([cc, term], axis=1)
    exchange(ctz, z, z_peer, side, 1)

    arrived(reqz.at[pl.ds(0, side - 1)], x_recv.at[0])
    row8 = iota((8, 128), 0)
    tile = reqz[0]
    for i in range(1, side):
        tile = jnp.where(row8 == i, reqz[i], tile)
    reqy[y] = tile
    exchange(reqy, y, y_peer, side, 2)

    def features(block, m):
        a = st[block, 0:16, pl.ds(pl.multiple_of(m * 128, 128), 128)]
        return a, 0.75 * jnp.sum(a * a, axis=0, keepdims=True)

    def put_right(block, m):
        b, norm = features(block, m)
        high, mid, low = thirds(b)
        parts = [high, mid, high, mid, low, high, norm_rows(norm, 0)]
        right[block * leaf_dev + m] = jnp.concatenate(parts, axis=0).T.astype(BF16)
        x = st[block, 16:24, pl.ds(pl.multiple_of(m * 128, 128), 128)]
        top = rounded(x)
        first = jnp.concatenate([top, x - top], axis=0)
        second = jnp.concatenate([top, jnp.zeros_like(top)], axis=0)
        weight[block * leaf_dev + m] = jnp.concatenate([first, second], axis=1).astype(BF16)

    def put_left(l):
        a, norm = features(1, l)
        high, mid, low = thirds(-1.5 * a)
        parts = [high, high, mid, mid, high, low, norm_rows(norm, 3)]
        left[l] = jnp.concatenate(parts, axis=0).astype(BF16)

    loop(0, leaf_dev, 4, put_left)
    loop(0, leaf_dev, 4, functools.partial(put_right, 1))

    arrived(ctz.at[pl.ds(0, side - 1)], x_recv.at[1])
    low_lanes = iota((8, 128), 1) < 64
    total = ctz[0]
    for i in range(1, side):
        total = total + ctz[i]
    for i in range(side // 2):
        cty[y, i] = jnp.where(low_lanes, ctz[2 * i], pltpu.roll(ctz[2 * i + 1], 64, 1))
    cty[y, side // 2] = total
    exchange(cty, y, y_peer, side, 3)

    arrived(reqy.at[pl.ds(0, side - 1)], x_recv.at[2])
    lane8 = iota((8, 128), 1)
    for i in range(side):
        asked = reqy[i]
        mine = (asked >> 4) == dev
        code = (lane8 * 16 + (asked & 15)).astype(F32)
        first = jnp.min(jnp.where(mine, code, 4096.0), axis=1, keepdims=True)
        last = jnp.max(jnp.where(mine, code, 0.0), axis=1, keepdims=True)
        ridx[i * 8 : (i + 1) * 8] = jnp.where(low_lanes, first, last).astype(I32) & 15

    def send_row(j):
        who = lax.rem(leaf + j, n_leaf)
        index = jnp.broadcast_to(ridx[pl.ds(who, 1), :], (8, 128))
        picked = coef2[0]
        for l in range(1, leaf_dev):
            picked = jnp.where(index == l, coef2[l], picked)
        rows_out[j - 1] = picked
        pltpu.make_async_remote_copy(
            src_ref=rows_out.at[j - 1],
            dst_ref=rows_in.at[j - 1],
            send_sem=x_send.at[5],
            recv_sem=x_recv.at[5],
            device_id=(grp, who),
            device_id_type=MESH,
        ).start()

    loop(1, n_leaf, 7, send_row)

    loads["cpl"].wait()

    def put_coupling(l):
        parts = [cpl_v[l, k] for k in range(far_two)]
        high, low = halves(jnp.concatenate(parts, axis=1))
        chi[l], clo[l] = high, low

    loop(0, leaf_dev, 4, put_coupling)

    arrived(cty.at[pl.ds(0, side - 1)], x_recv.at[3])
    total = cty[0, side // 2]
    for i in range(1, side):
        total = total + cty[i, side // 2]
    gcb[grp] = total
    exchange(gcb, grp, g_peer, n_grp, 4)

    for copy, block in zip(sides, (0, 2)):
        copy.wait_recv()
        loop(0, leaf_dev, 4, functools.partial(put_right, block))
    slots = near_s.shape[0]
    base = (dev - 1) * leaf_dev

    def near_leaf(l):
        target = left[l]
        count = count_s[l]
        acc = jnp.zeros((16, 128), F32)
        for k in range(slots):
            m = jnp.clip(near_s[k, l] - base, 0, 3 * leaf_dev - 1)
            gap = jnp.maximum(nn(right[m], target), 1e-30)
            u = gap * lax.rsqrt(gap)
            value = (1.0 + u) * jnp.exp(-u)
            high = value.astype(BF16)
            low = (value - high.astype(F32)).astype(BF16)
            live = jnp.where(k < count, 1.0, 0.0).astype(F32)
            part = nn(weight[m], jnp.concatenate([high, low], axis=0))
            acc = acc + live * part
        near_out[l] = fold(acc)

    loop(0, leaf_dev, 4, near_leaf)

    arrived(gcb.at[pl.ds(0, n_grp - 1)], x_recv.at[4])
    loads["cpc"].wait()
    loads["cpg"].wait()
    field_group = jnp.zeros((8, 64), F32)
    for h in range(n_grp):
        other = jnp.where(grp == h, 0.0, 1.0).astype(F32)
        gc = gcb[h][:, 64:] * other
        field_group = field_group + split_dot(nt, stack16(gc), cpg_v[0, h])
    field_cluster = split_dot(nt, stack16(field_group), upc_v[0])
    for k in range(cpc_v.shape[1]):
        f = jnp.clip(farc_s[0, k] - grp * n_leaf, 0, n_leaf - 1)
        fy, fz = lax.div(f, side), lax.rem(f, side)
        pair = cty[fy, lax.div(fz, 2)]
        flag = jnp.full((8, 128), lax.rem(fz, 2), I32)
        one = jnp.where(flag == 1, pltpu.roll(pair, 64, 1), pair)[:, :64]
        field_cluster = field_cluster + split_dot(nt, stack16(one), cpc_v[0, k])
    fc16 = stack16(field_cluster)
    for l in range(leaf_dev):
        down[l] = fold(nt(fc16, uhi[l]) + nt(fc16, ulo[l]))

    arrived(rows_in, x_recv.at[5])
    tab_copy.wait()
    for l in range(leaf_dev):
        chunks = []
        for pair in range(far_two // 2):
            both = []
            for half in range(2):
                t = tab_s[0, (2 * pair + half) * leaf_dev + l]
                got = rows_in[jnp.clip(t >> 1, 0, n_leaf - 2)]
                flag = jnp.full((8, 128), t & 1, I32)
                both.append(jnp.where(flag == half, got, pltpu.roll(got, 64, 1)))
            chunks.append(jnp.where(low_lanes, both[0], both[1]))
        x16 = stack16(jnp.concatenate(chunks, axis=1))
        field = fold(nt(x16, chi[l]) + nt(x16, clo[l])) + down[l]
        f16 = stack16(field)
        out_ref[:, l * 128 : (l + 1) * 128] = fold(nn(f16, bhi[l]) + nn(f16, blo[l])) + near_out[l]

    for copy in sides:
        copy.wait_send()
    for i, buf, n in ((0, reqz, side), (1, ctz, side), (2, reqy, side), (3, cty, side), (4, gcb, n_grp)):
        arrived(buf.at[pl.ds(0, n - 1)], x_send.at[i])
    arrived(rows_out, x_send.at[5])


def per_device(
    points,
    rhs,
    bases,
    up_leaf,
    up_cluster,
    coupling_leaf,
    coupling_cluster,
    coupling_group,
    near_list,
    near_count,
    far_leaf,
    far_cluster,
):
    n_leaf, n_grp = lax.axis_size("leaf"), lax.axis_size("grp")
    side = round(n_leaf**0.5)
    leaf_dev, rank, width = bases.shape
    nrhs = rhs.shape[0]
    far_two = far_leaf.shape[1]
    anywhere = pl.BlockSpec(memory_space=pltpu.HBM)
    scalars = pl.BlockSpec(memory_space=pltpu.SMEM)
    vmem = pltpu.VMEM
    return pl.pallas_call(
        functools.partial(kernel, side, n_grp),
        out_shape=vmem(rhs.shape, F32),
        in_specs=[scalars] * 3 + [anywhere] * 9,
        out_specs=pl.BlockSpec(memory_space=vmem),
        scratch_shapes=[
            vmem((3, 24, points.shape[1]), F32),
            vmem(bases.shape, F32),
            vmem(up_leaf.shape, F32),
            vmem(up_cluster.shape, F32),
            vmem(coupling_leaf.shape, F32),
            vmem(coupling_cluster.shape, F32),
            vmem(coupling_group.shape, F32),
            vmem(far_leaf.shape[::-1], I32),
            vmem(bases.shape, BF16),
            vmem(bases.shape, BF16),
            vmem(up_leaf.shape, BF16),
            vmem(up_leaf.shape, BF16),
            vmem((leaf_dev, rank, far_two * rank), BF16),
            vmem((leaf_dev, rank, far_two * rank), BF16),
            vmem((leaf_dev, width, 128), BF16),
            vmem((3 * leaf_dev, 128, width), BF16),
            vmem((3 * leaf_dev, 16, 2 * width), BF16),
            vmem((leaf_dev, nrhs, 128), F32),
            vmem((leaf_dev, nrhs, width), F32),
            vmem((leaf_dev, nrhs, rank), F32),
            vmem((1, 128), I32),
            pltpu.SMEM((1, 128), I32),
            vmem((n_leaf, 128), I32),
            vmem((side, 8, 128), I32),
            vmem((side, 8, 128), I32),
            vmem((side, 8, 128), F32),
            vmem((side, side // 2 + 1, 8, 128), F32),
            vmem((n_grp, 8, 128), F32),
            vmem((n_leaf - 1, 8, 128), F32),
            vmem((n_leaf - 1, 8, 128), F32),
            pltpu.SemaphoreType.DMA((9,)),
            pltpu.SemaphoreType.DMA,
            pltpu.SemaphoreType.DMA((2,)),
            pltpu.SemaphoreType.DMA((2,)),
            pltpu.SemaphoreType.DMA((6,)),
            pltpu.SemaphoreType.DMA((6,)),
        ],
        compiler_params=pltpu.CompilerParams(
            collective_id=0, has_side_effects=True, vmem_limit_bytes=32 * 1024 * 1024
        ),
    )(
        *(
            pltpu.with_memory_space_constraint(a, pltpu.HBM)
            for a in (
                near_list.T,
                near_count,
                far_cluster,
                points,
                rhs,
                bases,
                up_leaf,
                up_cluster,
                coupling_leaf,
                coupling_cluster,
                coupling_group,
                far_leaf.T,
            )
        )
    )


def solution(mesh):
    placed = (
        P(None, ("grp", "leaf")),
        P(None, ("grp", "leaf")),
        P(("grp", "leaf"), None, None),
        P(("grp", "leaf"), None, None),
        P(("grp", "leaf"), None, None),
        P(("grp", "leaf"), None, None, None),
        P(("grp", "leaf"), None, None, None),
        P("grp", None, None, None),
        P(("grp", "leaf"), None),
        P(("grp", "leaf")),
        P(("grp", "leaf"), None),
        P(("grp", "leaf"), None),
    )
    return jax.shard_map(
        per_device, mesh=mesh, in_specs=placed, out_specs=P(None, ("grp", "leaf")), check_vma=False
    )
```

```python
import functools

import jax
import jax.numpy as jnp
from jax import lax
from jax.experimental import pallas as pl
from jax.experimental.pallas import tpu as pltpu
from jax.sharding import PartitionSpec as P

F32, BF16, I32 = jnp.float32, jnp.bfloat16, jnp.int32
MESH = pl.DeviceIdType.MESH


def loop(start, stop, step, body):
    def some(i, c):
        for j in range(step):
            body(start + i * step + j)
        return c

    lax.fori_loop(0, (stop - start) // step, some, 0)


def iota(shape, dim):
    return lax.broadcasted_iota(I32, shape, dim)


def rounded(x):
    return x.astype(BF16).astype(F32)


def halves(x):
    high = x.astype(BF16)
    return high, (x - high.astype(F32)).astype(BF16)


def stack16(x):
    high = rounded(x)
    return jnp.concatenate([high, x - high], axis=0).astype(BF16)


def fold(x):
    return x[:8] + x[8:]


def nn(a, b):
    return lax.dot_general(a, b, (((1,), (0,)), ((), ())), preferred_element_type=F32)


def nt(a, b):
    return lax.dot_general(a, b, (((1,), (1,)), ((), ())), preferred_element_type=F32)


def split_dot(dot, x16, w):
    high, low = halves(w)
    return fold(dot(x16, high) + dot(x16, low))


def thirds(x):
    high = rounded(x)
    rest = x - high
    mid = rounded(rest)
    return high, mid, rest - mid


def norm_rows(norm, first):
    high, mid, low = thirds(norm)
    row = iota((32, norm.shape[1]), 0)
    at = row - first
    split = jnp.where(at == 0, high, jnp.where(at == 1, mid, jnp.where(at == 2, low, 0.0)))
    return jnp.where((row < 6) & ((at < 0) | (at > 2)), 1.0, split)


def kernel(
    side,
    n_grp,
    near_h,
    count_h,
    farc_h,
    pts_h,
    rhs_h,
    bases_h,
    upl_h,
    upc_h,
    cpl_h,
    cpc_h,
    cpg_h,
    farl_h,
    out_ref,
    near_s,
    count_s,
    farc_s,
    st,
    bases_v,
    upl_v,
    upc_v,
    cpl_v,
    cpc_v,
    cpg_v,
    farl_v,
    bhi,
    blo,
    vhi,
    vlo,
    whi,
    wlo,
    ghi,
    glo,
    left,
    right,
    weight,
    coef2,
    near_out,
    down,
    near_fc,
    tab_v,
    tab_s,
    ridx,
    ask,
    asked_by,
    ctz,
    cty,
    gcb,
    rows_out,
    rows_in,
    load_sem,
    tab_sem,
    st_send,
    st_recv,
    x_send,
    x_recv,
):
    n_leaf = side * side
    many = n_grp * n_leaf
    leaf_dev = bases_v.shape[0]
    grp, leaf = lax.axis_index("grp"), lax.axis_index("leaf")
    y, z = lax.div(leaf, side), lax.rem(leaf, side)
    dev = grp * n_leaf + leaf

    def at_dev(d):
        return lax.div(d, n_leaf), lax.rem(d, n_leaf)

    after, before = at_dev(lax.rem(dev + 1, many)), at_dev(lax.rem(dev + many - 1, many))

    barrier = pltpu.get_barrier_semaphore()

    def greet(who):
        pl.semaphore_signal(barrier, inc=1, device_id=who, device_id_type=MESH)

    greet(after)
    greet(before)

    loop(1, n_leaf, 7, lambda j: greet((grp, lax.rem(leaf + j, n_leaf))))
    loop(1, n_grp, 7, lambda j: greet((lax.rem(grp + j, n_grp), leaf)))

    loads = {}
    plan = (
        ("farl", farl_h, farl_v),
        ("pts", pts_h, st.at[1, pl.ds(0, 16)]),
        ("rhs", rhs_h, st.at[1, pl.ds(16, 8)]),
        ("bases", bases_h, bases_v),
        ("upl", upl_h, upl_v),
        ("upc", upc_h, upc_v),
        ("cpl", cpl_h, cpl_v),
        ("cpc", cpc_h, cpc_v),
        ("cpg", cpg_h, cpg_v),
        ("near", near_h, near_s),
        ("count", count_h, count_s),
        ("farc", farc_h, farc_s),
    )
    for i, (name, src, dst) in enumerate(plan):
        loads[name] = pltpu.make_async_copy(src, dst, load_sem.at[i])
        loads[name].start()

    def exchange(buf, at, peer, count, i):
        def go(j):
            pltpu.make_async_remote_copy(
                src_ref=buf.at[at],
                dst_ref=buf.at[at],
                send_sem=x_send.at[i],
                recv_sem=x_recv.at[i],
                device_id=peer(j),
                device_id_type=MESH,
            ).start()

        loop(1, count, 7, go)

    def arrived(ref, sem):
        pltpu.make_async_copy(ref, ref, sem).wait()

    def z_peer(j):
        return grp, y * side + lax.rem(z + j, side)

    def y_peer(j):
        return grp, lax.rem(y + j, side) * side + z

    def g_peer(j):
        return lax.rem(grp + j, n_grp), leaf

    loads["farl"].wait()
    far = farl_v[...]
    far_two = far.shape[0]
    asks = leaf_dev * far_two
    parts = [far[k : k + 1] for k in range(far_two)]
    row = jnp.concatenate([*parts, jnp.full((1, 128 - asks), -1, I32)], axis=1)
    ask[...] = row
    asked_by[pl.ds(leaf, 1)] = jnp.full((1, 128), -1, I32)
    owner = row >> 4
    lane_f, sub_f = iota((asks, 128), 1), iota((asks, 128), 0)
    spread = jnp.broadcast_to(owner.astype(F32), (asks, 128))
    column = jnp.sum(jnp.where(lane_f == sub_f, spread, 0.0), axis=1, keepdims=True)
    again = jnp.where((sub_f < lane_f) & (spread == column), 1.0, 0.0)
    again = jnp.max(again, axis=0, keepdims=True).astype(I32)
    place = ((leaf - (owner - grp * n_leaf)) & (n_leaf - 1)) - 1
    tab_v[...] = place * 2 + again
    tab_copy = pltpu.make_async_copy(tab_v, tab_s, tab_sem)
    tab_copy.start()

    loads["rhs"].wait()
    loads["bases"].wait()
    loads["upl"].wait()
    cc = jnp.zeros((16, 64), F32)
    for l in range(leaf_dev):
        x16 = stack16(st[1, 16:24, l * 128 : (l + 1) * 128])
        high, low = halves(bases_v[l])
        bhi[l], blo[l] = high, low
        two_high = jnp.concatenate([high, high], axis=0)
        two_low = jnp.concatenate([low, low], axis=0)
        c2 = fold(nt(x16, two_high) + nt(x16, two_low))
        coef2[l] = c2
        high, low = halves(upl_v[l])
        cc = cc + nn(stack16(c2), jnp.concatenate([high, low], axis=0))
    cc = fold(cc)
    loads["upc"].wait()
    term = split_dot(nn, stack16(cc), upc_v[0])
    ctz[z] = jnp.concatenate([cc, term], axis=1)

    loads["pts"].wait()
    pl.semaphore_wait(barrier, n_leaf + n_grp)

    def send_ask(j):
        pltpu.make_async_remote_copy(
            src_ref=ask,
            dst_ref=asked_by.at[pl.ds(leaf, 1)],
            send_sem=x_send.at[0],
            recv_sem=x_recv.at[0],
            device_id=(grp, lax.rem(leaf + j, n_leaf)),
            device_id_type=MESH,
        ).start()

    exchange(ctz, z, z_peer, side, 1)
    loop(1, n_leaf, 7, send_ask)
    def features(block, m):
        a = st[block, 0:16, pl.ds(pl.multiple_of(m * 128, 128), 128)]
        return a, 0.75 * jnp.sum(a * a, axis=0, keepdims=True)

    def put_right(block, m):
        b, norm = features(block, m)
        high, mid, low = thirds(b)
        parts = [high, mid, high, mid, low, high, norm_rows(norm, 0)]
        right[block * leaf_dev + m] = jnp.concatenate(parts, axis=0).T.astype(BF16)
        x = st[block, 16:24, pl.ds(pl.multiple_of(m * 128, 128), 128)]
        top = rounded(x)
        first = jnp.concatenate([top, x - top], axis=0)
        second = jnp.concatenate([top, jnp.zeros_like(top)], axis=0)
        weight[block * leaf_dev + m] = jnp.concatenate([first, second], axis=1).astype(BF16)

    def put_left(l):
        a, norm = features(1, l)
        high, mid, low = thirds(-1.5 * a)
        parts = [high, high, mid, mid, high, low, norm_rows(norm, 3)]
        left[l] = jnp.concatenate(parts, axis=0).astype(BF16)

    loop(0, leaf_dev, 4, put_left)
    loop(0, leaf_dev, 4, functools.partial(put_right, 1))
    sides = []
    for i, (who, slot) in enumerate(((after, 0), (before, 2))):
        copy = pltpu.make_async_remote_copy(
            src_ref=st.at[1],
            dst_ref=st.at[slot],
            send_sem=st_send.at[i],
            recv_sem=st_recv.at[i],
            device_id=who,
            device_id_type=MESH,
        )
        copy.start()
        sides.append(copy)


    loads["cpl"].wait()
    loads["cpg"].wait()

    def put_far(l):
        parts = [cpl_v[l, k] for k in range(far_two)]
        u = upl_v[l]
        parts += [u, jnp.zeros_like(u)]
        high, low = halves(jnp.concatenate(parts, axis=1))
        turned = jnp.concatenate([high, low], axis=0).T
        bh, bl = bhi[l], blo[l]
        both = nn(turned, jnp.concatenate([bh, bh], axis=0))
        both = both + nn(turned, jnp.concatenate([bl, bl], axis=0))
        high, low = halves(both)
        wide = far_two * 64
        vhi[l], vlo[l] = high[:wide], low[:wide]
        columns = pl.ds(pl.multiple_of(l * 128, 128), 128)
        whi[:, columns], wlo[:, columns] = high[wide : wide + 64], low[wide : wide + 64]

    loop(0, leaf_dev, 4, put_far)
    uc_high, uc_low = halves(upc_v[0])
    pieces = []
    for h in range(n_grp):
        high, low = halves(cpg_v[0, h])
        other = jnp.where(grp == h, 0.0, 1.0).astype(F32)
        pieces.append(other * (nn(uc_high, high) + nn(uc_high, low) + nn(uc_low, high)))
    ghi[...], glo[...] = halves(jnp.concatenate(pieces, axis=1))

    arrived(ctz.at[pl.ds(0, side - 1)], x_recv.at[1])
    low_lanes = iota((8, 128), 1) < 64
    total = ctz[0]
    for i in range(1, side):
        total = total + ctz[i]
    for i in range(side // 2):
        cty[y, i] = jnp.where(low_lanes, ctz[2 * i], pltpu.roll(ctz[2 * i + 1], 64, 1))
    cty[y, side // 2] = total
    exchange(cty, y, y_peer, side, 3)

    arrived(asked_by.at[pl.ds(0, n_leaf - 1)], x_recv.at[0])
    lane8 = iota((8, 128), 1)
    for i in range(n_leaf // 8):
        asked = asked_by[i * 8 : (i + 1) * 8]
        mine = (asked >> 4) == dev
        code = (lane8 * 16 + (asked & 15)).astype(F32)
        first = jnp.min(jnp.where(mine, code, 4096.0), axis=1, keepdims=True)
        last = jnp.max(jnp.where(mine, code, 0.0), axis=1, keepdims=True)
        ridx[i * 8 : (i + 1) * 8] = jnp.where(low_lanes, first, last).astype(I32) & 15

    def send_row(j):
        who = lax.rem(leaf + j, n_leaf)
        index = jnp.broadcast_to(ridx[pl.ds(who, 1), :], (8, 128))
        picked = coef2[0]
        for l in range(1, leaf_dev):
            picked = jnp.where(index == l, coef2[l], picked)
        rows_out[j - 1] = picked
        pltpu.make_async_remote_copy(
            src_ref=rows_out.at[j - 1],
            dst_ref=rows_in.at[j - 1],
            send_sem=x_send.at[5],
            recv_sem=x_recv.at[5],
            device_id=(grp, who),
            device_id_type=MESH,
        ).start()

    loop(1, n_leaf, 7, send_row)
    arrived(cty.at[pl.ds(0, side - 1)], x_recv.at[3])
    total = cty[0, side // 2]
    for i in range(1, side):
        total = total + cty[i, side // 2]
    gcb[grp] = jnp.where(low_lanes, pltpu.roll(total, 64, 1), total)
    exchange(gcb, grp, g_peer, n_grp, 4)

    loads["cpc"].wait()
    loads["farc"].wait()
    field_cluster = jnp.zeros((8, 64), F32)
    for k in range(cpc_v.shape[1]):
        f = jnp.clip(farc_s[0, k] - grp * n_leaf, 0, n_leaf - 1)
        fy, fz = lax.div(f, side), lax.rem(f, side)
        pair = cty[fy, lax.div(fz, 2)]
        flag = jnp.full((8, 128), lax.rem(fz, 2), I32)
        one = jnp.where(flag == 1, pltpu.roll(pair, 64, 1), pair)[:, :64]
        field_cluster = field_cluster + split_dot(nt, stack16(one), cpc_v[0, k])
    near_fc[...] = field_cluster

    for copy, block in zip(sides, (0, 2)):
        copy.wait_recv()
        loop(0, leaf_dev, 4, functools.partial(put_right, block))
    loads["near"].wait()
    loads["count"].wait()
    slots = near_s.shape[0]
    base = (dev - 1) * leaf_dev

    def near_leaf(l):
        target = left[l]
        count = count_s[l]
        acc = jnp.zeros((16, 128), F32)
        for k in range(slots):
            m = jnp.clip(near_s[k, l] - base, 0, 3 * leaf_dev - 1)
            gap = jnp.maximum(nn(right[m], target), 1e-30)
            u = gap * lax.rsqrt(gap)
            value = (1.0 + u) * jnp.exp(-u)
            high = value.astype(BF16)
            low = (value - high.astype(F32)).astype(BF16)
            live = jnp.where(k < count, 1.0, 0.0).astype(F32)
            part = nn(weight[m], jnp.concatenate([high, low], axis=0))
            acc = acc + live * part
        near_out[l] = fold(acc)

    loop(0, leaf_dev, 4, near_leaf)

    arrived(gcb.at[pl.ds(0, n_grp - 1)], x_recv.at[4])
    chunks = [jnp.where(low_lanes, gcb[2 * i], gcb[2 * i + 1]) for i in range(n_grp // 2)]
    x16 = stack16(jnp.concatenate(chunks, axis=1))
    fc16 = stack16(fold(nt(x16, ghi[...]) + nt(x16, glo[...])) + near_fc[...])
    down[...] = fold(nn(fc16, whi[...]) + nn(fc16, wlo[...]))

    arrived(rows_in, x_recv.at[5])
    tab_copy.wait()
    for l in range(leaf_dev):
        chunks = []
        for pair in range(far_two // 2):
            both = []
            for half in range(2):
                t = tab_s[0, (2 * pair + half) * leaf_dev + l]
                got = rows_in[jnp.clip(t >> 1, 0, n_leaf - 2)]
                flag = jnp.full((8, 128), t & 1, I32)
                both.append(jnp.where(flag == half, got, pltpu.roll(got, 64, 1)))
            chunks.append(jnp.where(low_lanes, both[0], both[1]))
        x16 = stack16(jnp.concatenate(chunks, axis=1))
        part = fold(nn(x16, vhi[l]) + nn(x16, vlo[l]))
        columns = slice(l * 128, (l + 1) * 128)
        out_ref[:, columns] = part + (down[:, columns] + near_out[l])

    for copy in sides:
        copy.wait_send()
    for i, buf, n in ((1, ctz, side), (3, cty, side), (4, gcb, n_grp)):
        arrived(buf.at[pl.ds(0, n - 1)], x_send.at[i])
    arrived(asked_by.at[pl.ds(0, n_leaf - 1)], x_send.at[0])
    arrived(rows_out, x_send.at[5])


def per_device(
    points,
    rhs,
    bases,
    up_leaf,
    up_cluster,
    coupling_leaf,
    coupling_cluster,
    coupling_group,
    near_list,
    near_count,
    far_leaf,
    far_cluster,
):
    n_leaf, n_grp = lax.axis_size("leaf"), lax.axis_size("grp")
    side = round(n_leaf**0.5)
    leaf_dev, rank, width = bases.shape
    nrhs = rhs.shape[0]
    far_two = far_leaf.shape[1]
    anywhere = pl.BlockSpec(memory_space=pltpu.HBM)
    vmem = pltpu.VMEM
    return pl.pallas_call(
        functools.partial(kernel, side, n_grp),
        out_shape=vmem(rhs.shape, F32),
        in_specs=[anywhere] * 12,
        out_specs=pl.BlockSpec(memory_space=vmem),
        scratch_shapes=[
            pltpu.SMEM(near_list.shape[::-1], I32),
            pltpu.SMEM(near_count.shape, I32),
            pltpu.SMEM(far_cluster.shape, I32),
            vmem((3, 24, points.shape[1]), F32),
            vmem(bases.shape, F32),
            vmem(up_leaf.shape, F32),
            vmem(up_cluster.shape, F32),
            vmem(coupling_leaf.shape, F32),
            vmem(coupling_cluster.shape, F32),
            vmem(coupling_group.shape, F32),
            vmem(far_leaf.shape[::-1], I32),
            vmem(bases.shape, BF16),
            vmem(bases.shape, BF16),
            vmem((leaf_dev, far_two * rank, width), BF16),
            vmem((leaf_dev, far_two * rank, width), BF16),
            vmem((rank, rhs.shape[1]), BF16),
            vmem((rank, rhs.shape[1]), BF16),
            vmem((rank, n_grp * rank), BF16),
            vmem((rank, n_grp * rank), BF16),
            vmem((leaf_dev, width, 128), BF16),
            vmem((3 * leaf_dev, 128, width), BF16),
            vmem((3 * leaf_dev, 16, 2 * width), BF16),
            vmem((leaf_dev, nrhs, 128), F32),
            vmem((leaf_dev, nrhs, width), F32),
            vmem(rhs.shape, F32),
            vmem((nrhs, rank), F32),
            vmem((1, 128), I32),
            pltpu.SMEM((1, 128), I32),
            vmem((n_leaf, 128), I32),
            vmem((1, 128), I32),
            vmem((n_leaf, 128), I32),
            vmem((side, 8, 128), F32),
            vmem((side, side // 2 + 1, 8, 128), F32),
            vmem((n_grp, 8, 128), F32),
            vmem((n_leaf - 1, 8, 128), F32),
            vmem((n_leaf - 1, 8, 128), F32),
            pltpu.SemaphoreType.DMA((12,)),
            pltpu.SemaphoreType.DMA,
            pltpu.SemaphoreType.DMA((2,)),
            pltpu.SemaphoreType.DMA((2,)),
            pltpu.SemaphoreType.DMA((6,)),
            pltpu.SemaphoreType.DMA((6,)),
        ],
        compiler_params=pltpu.CompilerParams(
            collective_id=0, has_side_effects=True, vmem_limit_bytes=32 * 1024 * 1024
        ),
    )(
        *(
            pltpu.with_memory_space_constraint(a, pltpu.HBM)
            for a in (
                near_list.T,
                near_count,
                far_cluster,
                points,
                rhs,
                bases,
                up_leaf,
                up_cluster,
                coupling_leaf,
                coupling_cluster,
                coupling_group,
                far_leaf.T,
            )
        )
    )


def solution(mesh):
    placed = (
        P(None, ("grp", "leaf")),
        P(None, ("grp", "leaf")),
        P(("grp", "leaf"), None, None),
        P(("grp", "leaf"), None, None),
        P(("grp", "leaf"), None, None),
        P(("grp", "leaf"), None, None, None),
        P(("grp", "leaf"), None, None, None),
        P("grp", None, None, None),
        P(("grp", "leaf"), None),
        P(("grp", "leaf")),
        P(("grp", "leaf"), None),
        P(("grp", "leaf"), None),
    )
    return jax.shard_map(
        per_device, mesh=mesh, in_specs=placed, out_specs=P(None, ("grp", "leaf")), check_vma=False
    )
```

```python
import functools

import jax
import jax.numpy as jnp
from jax import lax
from jax.experimental import pallas as pl
from jax.experimental.pallas import tpu as pltpu
from jax.sharding import PartitionSpec as P

F32, BF16, I32 = jnp.float32, jnp.bfloat16, jnp.int32
MESH = pl.DeviceIdType.MESH


def loop(start, stop, step, body):
    def some(i, c):
        for j in range(step):
            body(start + i * step + j)
        return c

    lax.fori_loop(0, (stop - start) // step, some, 0)


def iota(shape, dim):
    return lax.broadcasted_iota(I32, shape, dim)


def rounded(x):
    return x.astype(BF16).astype(F32)


def halves(x):
    high = x.astype(BF16)
    return high, (x - high.astype(F32)).astype(BF16)


def stack16(x):
    high = rounded(x)
    return jnp.concatenate([high, x - high], axis=0).astype(BF16)


def fold(x):
    return x[:8] + x[8:]


def nn(a, b):
    return lax.dot_general(a, b, (((1,), (0,)), ((), ())), preferred_element_type=F32)


def nt(a, b):
    return lax.dot_general(a, b, (((1,), (1,)), ((), ())), preferred_element_type=F32)


def split_dot(dot, x16, w):
    high, low = halves(w)
    return fold(dot(x16, high) + dot(x16, low))


def thirds(x):
    high = rounded(x)
    rest = x - high
    mid = rounded(rest)
    return high, mid, rest - mid


def norm_rows(norm, first):
    high, mid, low = thirds(norm)
    row = iota((32, norm.shape[1]), 0)
    at = row - first
    split = jnp.where(at == 0, high, jnp.where(at == 1, mid, jnp.where(at == 2, low, 0.0)))
    return jnp.where((row < 6) & ((at < 0) | (at > 2)), 1.0, split)


def kernel(
    side,
    n_grp,
    near_h,
    count_h,
    farc_h,
    pts_h,
    rhs_h,
    bases_h,
    upl_h,
    upc_h,
    cpl_h,
    cpc_h,
    cpg_h,
    farl_h,
    out_ref,
    near_s,
    count_s,
    farc_s,
    st,
    bases_v,
    upl_v,
    upc_v,
    cpl_v,
    cpc_v,
    cpg_v,
    farl_v,
    bhi,
    blo,
    vhi,
    vlo,
    whi,
    wlo,
    ghi,
    glo,
    left,
    right,
    weight,
    coef2,
    near_out,
    down,
    near_fc,
    tab_v,
    tab_s,
    ridx,
    ask,
    asked_by,
    ctz,
    cty,
    sums,
    gcb,
    rows_out,
    rows_in,
    load_sem,
    tab_sem,
    st_send,
    st_recv,
    x_send,
    x_recv,
):
    n_leaf = side * side
    many = n_grp * n_leaf
    leaf_dev = bases_v.shape[0]
    grp, leaf = lax.axis_index("grp"), lax.axis_index("leaf")
    y, z = lax.div(leaf, side), lax.rem(leaf, side)
    dev = grp * n_leaf + leaf

    def at_dev(d):
        return lax.div(d, n_leaf), lax.rem(d, n_leaf)

    after, before = at_dev(lax.rem(dev + 1, many)), at_dev(lax.rem(dev + many - 1, many))

    barrier = pltpu.get_barrier_semaphore()

    def greet(who):
        pl.semaphore_signal(barrier, inc=1, device_id=who, device_id_type=MESH)

    greet(after)
    greet(before)

    loop(1, n_leaf, 7, lambda j: greet((grp, lax.rem(leaf + j, n_leaf))))
    loop(1, n_grp, 7, lambda j: greet((lax.rem(grp + j, n_grp), leaf)))

    loads = {}
    plan = (
        ("farl", farl_h, farl_v),
        ("pts", pts_h, st.at[1, pl.ds(0, 16)]),
        ("rhs", rhs_h, st.at[1, pl.ds(16, 8)]),
        ("bases", bases_h, bases_v),
        ("upl", upl_h, upl_v),
        ("upc", upc_h, upc_v),
        ("cpl", cpl_h, cpl_v),
        ("cpc", cpc_h, cpc_v),
        ("cpg", cpg_h, cpg_v),
        ("near", near_h, near_s),
        ("count", count_h, count_s),
        ("farc", farc_h, farc_s),
    )
    for i, (name, src, dst) in enumerate(plan):
        loads[name] = pltpu.make_async_copy(src, dst, load_sem.at[i])
        loads[name].start()

    def exchange(buf, at, peer, count, i):
        def go(j):
            pltpu.make_async_remote_copy(
                src_ref=buf.at[at],
                dst_ref=buf.at[at],
                send_sem=x_send.at[i],
                recv_sem=x_recv.at[i],
                device_id=peer(j),
                device_id_type=MESH,
            ).start()

        loop(1, count, 7, go)

    def arrived(ref, sem):
        pltpu.make_async_copy(ref, ref, sem).wait()

    def z_peer(j):
        return grp, y * side + lax.rem(z + j, side)

    def y_peer(j):
        return grp, lax.rem(y + j, side) * side + z

    def g_peer(j):
        return lax.rem(grp + j, n_grp), leaf

    loads["farl"].wait()
    far = farl_v[...]
    far_two = far.shape[0]
    asks = leaf_dev * far_two
    parts = [far[k : k + 1] for k in range(far_two)]
    row = jnp.concatenate([*parts, jnp.full((1, 128 - asks), -1, I32)], axis=1)
    ask[...] = row
    asked_by[pl.ds(leaf, 1)] = jnp.full((1, 128), -1, I32)
    owner = row >> 4
    lane_f, sub_f = iota((asks, 128), 1), iota((asks, 128), 0)
    spread = jnp.broadcast_to(owner.astype(F32), (asks, 128))
    column = jnp.sum(jnp.where(lane_f == sub_f, spread, 0.0), axis=1, keepdims=True)
    again = jnp.where((sub_f < lane_f) & (spread == column), 1.0, 0.0)
    again = jnp.max(again, axis=0, keepdims=True).astype(I32)
    place = ((leaf - (owner - grp * n_leaf)) & (n_leaf - 1)) - 1
    tab_v[...] = place * 2 + again
    tab_copy = pltpu.make_async_copy(tab_v, tab_s, tab_sem)
    tab_copy.start()

    loads["rhs"].wait()
    loads["bases"].wait()
    loads["upl"].wait()
    cc = jnp.zeros((16, 64), F32)
    for l in range(leaf_dev):
        x16 = stack16(st[1, 16:24, l * 128 : (l + 1) * 128])
        high, low = halves(bases_v[l])
        bhi[l], blo[l] = high, low
        two_high = jnp.concatenate([high, high], axis=0)
        two_low = jnp.concatenate([low, low], axis=0)
        c2 = fold(nt(x16, two_high) + nt(x16, two_low))
        coef2[l] = c2
        high, low = halves(upl_v[l])
        cc = cc + nn(stack16(c2), jnp.concatenate([high, low], axis=0))
    cc = fold(cc)
    loads["upc"].wait()
    term = split_dot(nn, stack16(cc), upc_v[0])
    ctz[z] = jnp.concatenate([cc, term], axis=1)

    loads["pts"].wait()
    pl.semaphore_wait(barrier, n_leaf + n_grp)

    def send_ask(j):
        pltpu.make_async_remote_copy(
            src_ref=ask,
            dst_ref=asked_by.at[pl.ds(leaf, 1)],
            send_sem=x_send.at[0],
            recv_sem=x_recv.at[0],
            device_id=(grp, lax.rem(leaf + j, n_leaf)),
            device_id_type=MESH,
        ).start()

    exchange(ctz, z, z_peer, side, 1)
    loop(1, n_leaf, 7, send_ask)
    def features(block, m):
        a = st[block, 0:16, pl.ds(pl.multiple_of(m * 128, 128), 128)]
        return a, 0.75 * jnp.sum(a * a, axis=0, keepdims=True)

    def put_right(block, m):
        b, norm = features(block, m)
        high, mid, low = thirds(b)
        parts = [high, mid, high, mid, low, high, norm_rows(norm, 0)]
        right[block * leaf_dev + m] = jnp.concatenate(parts, axis=0).T.astype(BF16)
        x = st[block, 16:24, pl.ds(pl.multiple_of(m * 128, 128), 128)]
        top = rounded(x)
        first = jnp.concatenate([top, x - top], axis=0)
        second = jnp.concatenate([top, jnp.zeros_like(top)], axis=0)
        weight[block * leaf_dev + m] = jnp.concatenate([first, second], axis=1).astype(BF16)

    def put_left(l):
        a, norm = features(1, l)
        high, mid, low = thirds(-1.5 * a)
        parts = [high, high, mid, mid, high, low, norm_rows(norm, 3)]
        left[l] = jnp.concatenate(parts, axis=0).astype(BF16)

    loop(0, leaf_dev, 4, put_left)
    loop(0, leaf_dev, 4, functools.partial(put_right, 1))
    sides = []
    for i, (who, slot) in enumerate(((after, 0), (before, 2))):
        copy = pltpu.make_async_remote_copy(
            src_ref=st.at[1],
            dst_ref=st.at[slot],
            send_sem=st_send.at[i],
            recv_sem=st_recv.at[i],
            device_id=who,
            device_id_type=MESH,
        )
        copy.start()
        sides.append(copy)


    loads["cpl"].wait()
    loads["cpg"].wait()

    def put_far(l):
        parts = [cpl_v[l, k] for k in range(far_two)]
        u = upl_v[l]
        parts += [u, jnp.zeros_like(u)]
        high, low = halves(jnp.concatenate(parts, axis=1))
        turned = jnp.concatenate([high, low], axis=0).T
        bh, bl = bhi[l], blo[l]
        both = nn(turned, jnp.concatenate([bh, bh], axis=0))
        both = both + nn(turned, jnp.concatenate([bl, bl], axis=0))
        high, low = halves(both)
        wide = far_two * 64
        vhi[l], vlo[l] = high[:wide], low[:wide]
        columns = pl.ds(pl.multiple_of(l * 128, 128), 128)
        whi[:, columns], wlo[:, columns] = high[wide : wide + 64], low[wide : wide + 64]

    loop(0, leaf_dev, 4, put_far)
    uc_high, uc_low = halves(upc_v[0])
    pieces = []
    for h in range(n_grp):
        high, low = halves(cpg_v[0, h])
        other = jnp.where(grp == h, 0.0, 1.0).astype(F32)
        pieces.append(other * (nn(uc_high, high) + nn(uc_high, low) + nn(uc_low, high)))
    ghi[...], glo[...] = halves(jnp.concatenate(pieces, axis=1))

    arrived(ctz.at[pl.ds(0, side - 1)], x_recv.at[1])
    low_lanes = iota((8, 128), 1) < 64
    total = ctz[0]
    for i in range(1, side):
        total = total + ctz[i]
    sums[y] = total
    exchange(sums, y, y_peer, side, 2)
    for i in range(side // 2):
        cty[y, i] = jnp.where(low_lanes, ctz[2 * i], pltpu.roll(ctz[2 * i + 1], 64, 1))
    exchange(cty, y, y_peer, side, 3)

    arrived(asked_by.at[pl.ds(0, n_leaf - 1)], x_recv.at[0])
    lane8 = iota((8, 128), 1)
    for i in range(n_leaf // 8):
        asked = asked_by[i * 8 : (i + 1) * 8]
        mine = (asked >> 4) == dev
        code = (lane8 * 16 + (asked & 15)).astype(F32)
        first = jnp.min(jnp.where(mine, code, 4096.0), axis=1, keepdims=True)
        last = jnp.max(jnp.where(mine, code, 0.0), axis=1, keepdims=True)
        ridx[i * 8 : (i + 1) * 8] = jnp.where(low_lanes, first, last).astype(I32) & 15

    def send_row(j):
        who = lax.rem(leaf + j, n_leaf)
        index = jnp.broadcast_to(ridx[pl.ds(who, 1), :], (8, 128))
        picked = coef2[0]
        for l in range(1, leaf_dev):
            picked = jnp.where(index == l, coef2[l], picked)
        rows_out[j - 1] = picked
        pltpu.make_async_remote_copy(
            src_ref=rows_out.at[j - 1],
            dst_ref=rows_in.at[j - 1],
            send_sem=x_send.at[5],
            recv_sem=x_recv.at[5],
            device_id=(grp, who),
            device_id_type=MESH,
        ).start()

    loop(1, n_leaf, 7, send_row)
    arrived(sums.at[pl.ds(0, side - 1)], x_recv.at[2])
    total = sums[0]
    for i in range(1, side):
        total = total + sums[i]
    gcb[grp] = jnp.where(low_lanes, pltpu.roll(total, 64, 1), total)
    exchange(gcb, grp, g_peer, n_grp, 4)

    for copy, block in zip(sides, (0, 2)):
        copy.wait_recv()
        loop(0, leaf_dev, 4, functools.partial(put_right, block))
    loads["near"].wait()
    loads["count"].wait()
    slots = near_s.shape[0]
    base = (dev - 1) * leaf_dev

    def near_leaf(l):
        target = left[l]
        count = count_s[l]
        acc = jnp.zeros((16, 128), F32)
        for k in range(slots):
            m = jnp.clip(near_s[k, l] - base, 0, 3 * leaf_dev - 1)
            gap = jnp.maximum(nn(right[m], target), 1e-30)
            u = gap * lax.rsqrt(gap)
            value = (1.0 + u) * jnp.exp(-u)
            high = value.astype(BF16)
            low = (value - high.astype(F32)).astype(BF16)
            live = jnp.where(k < count, 1.0, 0.0).astype(F32)
            part = nn(weight[m], jnp.concatenate([high, low], axis=0))
            acc = acc + live * part
        near_out[l] = fold(acc)

    loop(0, leaf_dev, 4, near_leaf)

    arrived(cty.at[pl.ds(0, side - 1)], x_recv.at[3])
    loads["cpc"].wait()
    loads["farc"].wait()
    field_cluster = jnp.zeros((8, 64), F32)
    for k in range(cpc_v.shape[1]):
        f = jnp.clip(farc_s[0, k] - grp * n_leaf, 0, n_leaf - 1)
        fy, fz = lax.div(f, side), lax.rem(f, side)
        pair = cty[fy, lax.div(fz, 2)]
        flag = jnp.full((8, 128), lax.rem(fz, 2), I32)
        one = jnp.where(flag == 1, pltpu.roll(pair, 64, 1), pair)[:, :64]
        field_cluster = field_cluster + split_dot(nt, stack16(one), cpc_v[0, k])
    near_fc[...] = field_cluster

    arrived(gcb.at[pl.ds(0, n_grp - 1)], x_recv.at[4])
    chunks = [jnp.where(low_lanes, gcb[2 * i], gcb[2 * i + 1]) for i in range(n_grp // 2)]
    x16 = stack16(jnp.concatenate(chunks, axis=1))
    fc16 = stack16(fold(nt(x16, ghi[...]) + nt(x16, glo[...])) + near_fc[...])
    down[...] = fold(nn(fc16, whi[...]) + nn(fc16, wlo[...]))

    arrived(rows_in, x_recv.at[5])
    tab_copy.wait()
    for l in range(leaf_dev):
        chunks = []
        for pair in range(far_two // 2):
            both = []
            for half in range(2):
                t = tab_s[0, (2 * pair + half) * leaf_dev + l]
                got = rows_in[jnp.clip(t >> 1, 0, n_leaf - 2)]
                flag = jnp.full((8, 128), t & 1, I32)
                both.append(jnp.where(flag == half, got, pltpu.roll(got, 64, 1)))
            chunks.append(jnp.where(low_lanes, both[0], both[1]))
        x16 = stack16(jnp.concatenate(chunks, axis=1))
        part = fold(nn(x16, vhi[l]) + nn(x16, vlo[l]))
        columns = slice(l * 128, (l + 1) * 128)
        out_ref[:, columns] = part + (down[:, columns] + near_out[l])

    for copy in sides:
        copy.wait_send()
    for i, buf, n in ((1, ctz, side), (2, sums, side), (3, cty, side), (4, gcb, n_grp)):
        arrived(buf.at[pl.ds(0, n - 1)], x_send.at[i])
    arrived(asked_by.at[pl.ds(0, n_leaf - 1)], x_send.at[0])
    arrived(rows_out, x_send.at[5])


def per_device(
    points,
    rhs,
    bases,
    up_leaf,
    up_cluster,
    coupling_leaf,
    coupling_cluster,
    coupling_group,
    near_list,
    near_count,
    far_leaf,
    far_cluster,
):
    n_leaf, n_grp = lax.axis_size("leaf"), lax.axis_size("grp")
    side = round(n_leaf**0.5)
    leaf_dev, rank, width = bases.shape
    nrhs = rhs.shape[0]
    far_two = far_leaf.shape[1]
    anywhere = pl.BlockSpec(memory_space=pltpu.HBM)
    vmem = pltpu.VMEM
    return pl.pallas_call(
        functools.partial(kernel, side, n_grp),
        out_shape=vmem(rhs.shape, F32),
        in_specs=[anywhere] * 12,
        out_specs=pl.BlockSpec(memory_space=vmem),
        scratch_shapes=[
            pltpu.SMEM(near_list.shape[::-1], I32),
            pltpu.SMEM(near_count.shape, I32),
            pltpu.SMEM(far_cluster.shape, I32),
            vmem((3, 24, points.shape[1]), F32),
            vmem(bases.shape, F32),
            vmem(up_leaf.shape, F32),
            vmem(up_cluster.shape, F32),
            vmem(coupling_leaf.shape, F32),
            vmem(coupling_cluster.shape, F32),
            vmem(coupling_group.shape, F32),
            vmem(far_leaf.shape[::-1], I32),
            vmem(bases.shape, BF16),
            vmem(bases.shape, BF16),
            vmem((leaf_dev, far_two * rank, width), BF16),
            vmem((leaf_dev, far_two * rank, width), BF16),
            vmem((rank, rhs.shape[1]), BF16),
            vmem((rank, rhs.shape[1]), BF16),
            vmem((rank, n_grp * rank), BF16),
            vmem((rank, n_grp * rank), BF16),
            vmem((leaf_dev, width, 128), BF16),
            vmem((3 * leaf_dev, 128, width), BF16),
            vmem((3 * leaf_dev, 16, 2 * width), BF16),
            vmem((leaf_dev, nrhs, 128), F32),
            vmem((leaf_dev, nrhs, width), F32),
            vmem(rhs.shape, F32),
            vmem((nrhs, rank), F32),
            vmem((1, 128), I32),
            pltpu.SMEM((1, 128), I32),
            vmem((n_leaf, 128), I32),
            vmem((1, 128), I32),
            vmem((n_leaf, 128), I32),
            vmem((side, 8, 128), F32),
            vmem((side, side // 2, 8, 128), F32),
            vmem((side, 8, 128), F32),
            vmem((n_grp, 8, 128), F32),
            vmem((n_leaf - 1, 8, 128), F32),
            vmem((n_leaf - 1, 8, 128), F32),
            pltpu.SemaphoreType.DMA((12,)),
            pltpu.SemaphoreType.DMA,
            pltpu.SemaphoreType.DMA((2,)),
            pltpu.SemaphoreType.DMA((2,)),
            pltpu.SemaphoreType.DMA((6,)),
            pltpu.SemaphoreType.DMA((6,)),
        ],
        compiler_params=pltpu.CompilerParams(
            collective_id=0, has_side_effects=True, vmem_limit_bytes=32 * 1024 * 1024
        ),
    )(
        *(
            pltpu.with_memory_space_constraint(a, pltpu.HBM)
            for a in (
                near_list.T,
                near_count,
                far_cluster,
                points,
                rhs,
                bases,
                up_leaf,
                up_cluster,
                coupling_leaf,
                coupling_cluster,
                coupling_group,
                far_leaf.T,
            )
        )
    )


def solution(mesh):
    placed = (
        P(None, ("grp", "leaf")),
        P(None, ("grp", "leaf")),
        P(("grp", "leaf"), None, None),
        P(("grp", "leaf"), None, None),
        P(("grp", "leaf"), None, None),
        P(("grp", "leaf"), None, None, None),
        P(("grp", "leaf"), None, None, None),
        P("grp", None, None, None),
        P(("grp", "leaf"), None),
        P(("grp", "leaf")),
        P(("grp", "leaf"), None),
        P(("grp", "leaf"), None),
    )
    return jax.shard_map(
        per_device, mesh=mesh, in_specs=placed, out_specs=P(None, ("grp", "leaf")), check_vma=False
    )
```

```python
import functools

import jax
import jax.numpy as jnp
from jax import lax
from jax.experimental import pallas as pl
from jax.experimental.pallas import tpu as pltpu
from jax.sharding import PartitionSpec as P

F32, BF16, I32 = jnp.float32, jnp.bfloat16, jnp.int32
MESH = pl.DeviceIdType.MESH


def loop(start, stop, step, body):
    def some(i, c):
        for j in range(step):
            body(start + i * step + j)
        return c

    lax.fori_loop(0, (stop - start) // step, some, 0)


def iota(shape, dim):
    return lax.broadcasted_iota(I32, shape, dim)


def rounded(x):
    return x.astype(BF16).astype(F32)


def halves(x):
    high = x.astype(BF16)
    return high, (x - high.astype(F32)).astype(BF16)


def stack16(x):
    high = rounded(x)
    return jnp.concatenate([high, x - high], axis=0).astype(BF16)


def fold(x):
    return x[:8] + x[8:]


def nn(a, b):
    return lax.dot_general(a, b, (((1,), (0,)), ((), ())), preferred_element_type=F32)


def nt(a, b):
    return lax.dot_general(a, b, (((1,), (1,)), ((), ())), preferred_element_type=F32)


def split_dot(dot, x16, w):
    high, low = halves(w)
    return fold(dot(x16, high) + dot(x16, low))


def thirds(x):
    high = rounded(x)
    rest = x - high
    mid = rounded(rest)
    return high, mid, rest - mid


def norm_rows(norm, first):
    high, mid, low = thirds(norm)
    row = iota((32, norm.shape[1]), 0)
    at = row - first
    split = jnp.where(at == 0, high, jnp.where(at == 1, mid, jnp.where(at == 2, low, 0.0)))
    return jnp.where((row < 6) & ((at < 0) | (at > 2)), 1.0, split)


def kernel(
    side,
    n_grp,
    near_h,
    count_h,
    farc_h,
    pts_h,
    rhs_h,
    bases_h,
    upl_h,
    upc_h,
    cpl_h,
    cpc_h,
    cpg_h,
    farl_h,
    out_ref,
    near_s,
    count_s,
    farc_s,
    st,
    bases_v,
    upl_v,
    upc_v,
    cpl_v,
    cpc_v,
    cpg_v,
    farl_v,
    bhi,
    blo,
    vhi,
    vlo,
    whi,
    wlo,
    ghi,
    glo,
    left,
    right,
    weight,
    coef2,
    near_out,
    down,
    near_fc,
    tab_v,
    tab_s,
    ridx,
    ask,
    asked_by,
    ctz,
    cty,
    sums,
    gcb,
    rows_out,
    rows_in,
    load_sem,
    tab_sem,
    st_send,
    st_recv,
    x_send,
    x_recv,
):
    n_leaf = side * side
    many = n_grp * n_leaf
    leaf_dev = bases_v.shape[0]
    grp, leaf = lax.axis_index("grp"), lax.axis_index("leaf")
    y, z = lax.div(leaf, side), lax.rem(leaf, side)
    dev = grp * n_leaf + leaf

    def at_dev(d):
        return lax.div(d, n_leaf), lax.rem(d, n_leaf)

    after, before = at_dev(lax.rem(dev + 1, many)), at_dev(lax.rem(dev + many - 1, many))

    loads = {}
    plan = (
        ("farl", farl_h, farl_v),
        ("pts", pts_h, st.at[1, pl.ds(0, 16)]),
        ("rhs", rhs_h, st.at[1, pl.ds(16, 8)]),
        ("bases", bases_h, bases_v),
        ("upl", upl_h, upl_v),
        ("upc", upc_h, upc_v),
        ("cpl", cpl_h, cpl_v),
        ("cpc", cpc_h, cpc_v),
        ("cpg", cpg_h, cpg_v),
        ("near", near_h, near_s),
        ("count", count_h, count_s),
        ("farc", farc_h, farc_s),
    )
    for i, (name, src, dst) in enumerate(plan):
        loads[name] = pltpu.make_async_copy(src, dst, load_sem.at[i])
    first = ("rhs", "bases", "upl", "farl", "upc")
    for name in first:
        loads[name].start()


    barrier = pltpu.get_barrier_semaphore()

    def greet(who):
        pl.semaphore_signal(barrier, inc=1, device_id=who, device_id_type=MESH)

    greet(after)
    greet(before)

    loop(1, n_leaf, 7, lambda j: greet((grp, lax.rem(leaf + j, n_leaf))))
    loop(1, n_grp, 7, lambda j: greet((lax.rem(grp + j, n_grp), leaf)))

    for name, copy in loads.items():
        if name not in first:
            copy.start()

    def exchange(buf, at, peer, count, i):
        def go(j):
            pltpu.make_async_remote_copy(
                src_ref=buf.at[at],
                dst_ref=buf.at[at],
                send_sem=x_send.at[i],
                recv_sem=x_recv.at[i],
                device_id=peer(j),
                device_id_type=MESH,
            ).start()

        loop(1, count, 7, go)

    def arrived(ref, sem):
        pltpu.make_async_copy(ref, ref, sem).wait()

    def z_peer(j):
        return grp, y * side + lax.rem(z + j, side)

    def y_peer(j):
        return grp, lax.rem(y + j, side) * side + z

    def g_peer(j):
        return lax.rem(grp + j, n_grp), leaf

    loads["farl"].wait()
    far = farl_v[...]
    far_two = far.shape[0]
    asks = leaf_dev * far_two
    parts = [far[k : k + 1] for k in range(far_two)]
    row = jnp.concatenate([*parts, jnp.full((1, 128 - asks), -1, I32)], axis=1)
    ask[...] = row
    asked_by[pl.ds(leaf, 1)] = jnp.full((1, 128), -1, I32)
    owner = row >> 4
    lane_f, sub_f = iota((asks, 128), 1), iota((asks, 128), 0)
    spread = jnp.broadcast_to(owner.astype(F32), (asks, 128))
    column = jnp.sum(jnp.where(lane_f == sub_f, spread, 0.0), axis=1, keepdims=True)
    again = jnp.where((sub_f < lane_f) & (spread == column), 1.0, 0.0)
    again = jnp.max(again, axis=0, keepdims=True).astype(I32)
    place = ((leaf - (owner - grp * n_leaf)) & (n_leaf - 1)) - 1
    tab_v[...] = place * 2 + again
    tab_copy = pltpu.make_async_copy(tab_v, tab_s, tab_sem)
    tab_copy.start()

    loads["rhs"].wait()
    loads["bases"].wait()
    loads["upl"].wait()
    cc = jnp.zeros((16, 64), F32)
    for l in range(leaf_dev):
        x16 = stack16(st[1, 16:24, l * 128 : (l + 1) * 128])
        high, low = halves(bases_v[l])
        bhi[l], blo[l] = high, low
        two_high = jnp.concatenate([high, high], axis=0)
        two_low = jnp.concatenate([low, low], axis=0)
        c2 = fold(nt(x16, two_high) + nt(x16, two_low))
        coef2[l] = c2
        high, low = halves(upl_v[l])
        cc = cc + nn(stack16(c2), jnp.concatenate([high, low], axis=0))
    cc = fold(cc)
    loads["upc"].wait()
    term = split_dot(nn, stack16(cc), upc_v[0])
    ctz[z] = jnp.concatenate([cc, term], axis=1)

    loads["pts"].wait()
    pl.semaphore_wait(barrier, n_leaf + n_grp)

    def send_ask(j):
        pltpu.make_async_remote_copy(
            src_ref=ask,
            dst_ref=asked_by.at[pl.ds(leaf, 1)],
            send_sem=x_send.at[0],
            recv_sem=x_recv.at[0],
            device_id=(grp, lax.rem(leaf + j, n_leaf)),
            device_id_type=MESH,
        ).start()

    exchange(ctz, z, z_peer, side, 1)
    loop(1, n_leaf, 7, send_ask)
    def features(block, m):
        a = st[block, 0:16, pl.ds(pl.multiple_of(m * 128, 128), 128)]
        return a, 0.75 * jnp.sum(a * a, axis=0, keepdims=True)

    def put_right(block, m):
        b, norm = features(block, m)
        high, mid, low = thirds(b)
        parts = [high, mid, high, mid, low, high, norm_rows(norm, 0)]
        right[block * leaf_dev + m] = jnp.concatenate(parts, axis=0).T.astype(BF16)
        x = st[block, 16:24, pl.ds(pl.multiple_of(m * 128, 128), 128)]
        top = rounded(x)
        first = jnp.concatenate([top, x - top], axis=0)
        second = jnp.concatenate([top, jnp.zeros_like(top)], axis=0)
        weight[block * leaf_dev + m] = jnp.concatenate([first, second], axis=1).astype(BF16)

    def put_left(l):
        a, norm = features(1, l)
        high, mid, low = thirds(-1.5 * a)
        parts = [high, high, mid, mid, high, low, norm_rows(norm, 3)]
        left[l] = jnp.concatenate(parts, axis=0).astype(BF16)

    loop(0, leaf_dev, 4, put_left)
    loop(0, leaf_dev, 4, functools.partial(put_right, 1))
    sides = []
    for i, (who, slot) in enumerate(((after, 0), (before, 2))):
        copy = pltpu.make_async_remote_copy(
            src_ref=st.at[1],
            dst_ref=st.at[slot],
            send_sem=st_send.at[i],
            recv_sem=st_recv.at[i],
            device_id=who,
            device_id_type=MESH,
        )
        copy.start()
        sides.append(copy)


    loads["cpl"].wait()
    loads["cpg"].wait()

    def put_far(l):
        parts = [cpl_v[l, k] for k in range(far_two)]
        u = upl_v[l]
        parts += [u, jnp.zeros_like(u)]
        high, low = halves(jnp.concatenate(parts, axis=1))
        turned = jnp.concatenate([high, low], axis=0).T
        bh, bl = bhi[l], blo[l]
        both = nn(turned, jnp.concatenate([bh, bh], axis=0))
        both = both + nn(turned, jnp.concatenate([bl, bl], axis=0))
        high, low = halves(both)
        wide = far_two * 64
        vhi[l], vlo[l] = high[:wide], low[:wide]
        columns = pl.ds(pl.multiple_of(l * 128, 128), 128)
        whi[:, columns], wlo[:, columns] = high[wide : wide + 64], low[wide : wide + 64]

    loop(0, leaf_dev, 4, put_far)
    uc_high, uc_low = halves(upc_v[0])
    pieces = []
    for h in range(n_grp):
        high, low = halves(cpg_v[0, h])
        other = jnp.where(grp == h, 0.0, 1.0).astype(F32)
        pieces.append(other * (nn(uc_high, high) + nn(uc_high, low) + nn(uc_low, high)))
    ghi[...], glo[...] = halves(jnp.concatenate(pieces, axis=1))

    arrived(ctz.at[pl.ds(0, side - 1)], x_recv.at[1])
    low_lanes = iota((8, 128), 1) < 64
    total = ctz[0]
    for i in range(1, side):
        total = total + ctz[i]
    sums[y] = total
    exchange(sums, y, y_peer, side, 2)
    for i in range(side // 2):
        cty[y, i] = jnp.where(low_lanes, ctz[2 * i], pltpu.roll(ctz[2 * i + 1], 64, 1))
    exchange(cty, y, y_peer, side, 3)

    arrived(asked_by.at[pl.ds(0, n_leaf - 1)], x_recv.at[0])
    lane8 = iota((8, 128), 1)
    for i in range(n_leaf // 8):
        asked = asked_by[i * 8 : (i + 1) * 8]
        mine = (asked >> 4) == dev
        code = (lane8 * 16 + (asked & 15)).astype(F32)
        first = jnp.min(jnp.where(mine, code, 4096.0), axis=1, keepdims=True)
        last = jnp.max(jnp.where(mine, code, 0.0), axis=1, keepdims=True)
        ridx[i * 8 : (i + 1) * 8] = jnp.where(low_lanes, first, last).astype(I32) & 15

    def send_row(j):
        who = lax.rem(leaf + j, n_leaf)
        index = jnp.broadcast_to(ridx[pl.ds(who, 1), :], (8, 128))
        picked = coef2[0]
        for l in range(1, leaf_dev):
            picked = jnp.where(index == l, coef2[l], picked)
        rows_out[j - 1] = picked
        pltpu.make_async_remote_copy(
            src_ref=rows_out.at[j - 1],
            dst_ref=rows_in.at[j - 1],
            send_sem=x_send.at[5],
            recv_sem=x_recv.at[5],
            device_id=(grp, who),
            device_id_type=MESH,
        ).start()

    loop(1, n_leaf, 7, send_row)
    arrived(sums.at[pl.ds(0, side - 1)], x_recv.at[2])
    total = sums[0]
    for i in range(1, side):
        total = total + sums[i]
    gcb[grp] = jnp.where(low_lanes, pltpu.roll(total, 64, 1), total)
    exchange(gcb, grp, g_peer, n_grp, 4)

    for copy, block in zip(sides, (0, 2)):
        copy.wait_recv()
        loop(0, leaf_dev, 4, functools.partial(put_right, block))
    loads["near"].wait()
    loads["count"].wait()
    slots = near_s.shape[0]
    base = (dev - 1) * leaf_dev

    def near_leaf(l):
        target = left[l]
        count = count_s[l]
        acc = jnp.zeros((16, 128), F32)
        for k in range(slots):
            m = jnp.clip(near_s[k, l] - base, 0, 3 * leaf_dev - 1)
            gap = jnp.maximum(nn(right[m], target), 1e-30)
            u = gap * lax.rsqrt(gap)
            value = (1.0 + u) * jnp.exp(-u)
            high = value.astype(BF16)
            low = (value - high.astype(F32)).astype(BF16)
            live = jnp.where(k < count, 1.0, 0.0).astype(F32)
            part = nn(weight[m], jnp.concatenate([high, low], axis=0))
            acc = acc + live * part
        near_out[l] = fold(acc)

    loop(0, leaf_dev, 4, near_leaf)

    arrived(cty.at[pl.ds(0, side - 1)], x_recv.at[3])
    loads["cpc"].wait()
    loads["farc"].wait()
    field_cluster = jnp.zeros((8, 64), F32)
    for k in range(cpc_v.shape[1]):
        f = jnp.clip(farc_s[0, k] - grp * n_leaf, 0, n_leaf - 1)
        fy, fz = lax.div(f, side), lax.rem(f, side)
        pair = cty[fy, lax.div(fz, 2)]
        flag = jnp.full((8, 128), lax.rem(fz, 2), I32)
        one = jnp.where(flag == 1, pltpu.roll(pair, 64, 1), pair)[:, :64]
        field_cluster = field_cluster + split_dot(nt, stack16(one), cpc_v[0, k])
    near_fc[...] = field_cluster

    arrived(gcb.at[pl.ds(0, n_grp - 1)], x_recv.at[4])
    chunks = [jnp.where(low_lanes, gcb[2 * i], gcb[2 * i + 1]) for i in range(n_grp // 2)]
    x16 = stack16(jnp.concatenate(chunks, axis=1))
    fc16 = stack16(fold(nt(x16, ghi[...]) + nt(x16, glo[...])) + near_fc[...])
    down[...] = fold(nn(fc16, whi[...]) + nn(fc16, wlo[...]))

    arrived(rows_in, x_recv.at[5])
    tab_copy.wait()
    for l in range(leaf_dev):
        chunks = []
        for pair in range(far_two // 2):
            both = []
            for half in range(2):
                t = tab_s[0, (2 * pair + half) * leaf_dev + l]
                got = rows_in[jnp.clip(t >> 1, 0, n_leaf - 2)]
                flag = jnp.full((8, 128), t & 1, I32)
                both.append(jnp.where(flag == half, got, pltpu.roll(got, 64, 1)))
            chunks.append(jnp.where(low_lanes, both[0], both[1]))
        x16 = stack16(jnp.concatenate(chunks, axis=1))
        part = fold(nn(x16, vhi[l]) + nn(x16, vlo[l]))
        columns = slice(l * 128, (l + 1) * 128)
        out_ref[:, columns] = part + (down[:, columns] + near_out[l])

    for copy in sides:
        copy.wait_send()
    for i, buf, n in ((1, ctz, side), (2, sums, side), (3, cty, side), (4, gcb, n_grp)):
        arrived(buf.at[pl.ds(0, n - 1)], x_send.at[i])
    arrived(asked_by.at[pl.ds(0, n_leaf - 1)], x_send.at[0])
    arrived(rows_out, x_send.at[5])


def per_device(
    points,
    rhs,
    bases,
    up_leaf,
    up_cluster,
    coupling_leaf,
    coupling_cluster,
    coupling_group,
    near_list,
    near_count,
    far_leaf,
    far_cluster,
):
    n_leaf, n_grp = lax.axis_size("leaf"), lax.axis_size("grp")
    side = round(n_leaf**0.5)
    leaf_dev, rank, width = bases.shape
    nrhs = rhs.shape[0]
    far_two = far_leaf.shape[1]
    anywhere = pl.BlockSpec(memory_space=pltpu.HBM)
    vmem = pltpu.VMEM
    return pl.pallas_call(
        functools.partial(kernel, side, n_grp),
        out_shape=vmem(rhs.shape, F32),
        in_specs=[anywhere] * 12,
        out_specs=pl.BlockSpec(memory_space=vmem),
        scratch_shapes=[
            pltpu.SMEM(near_list.shape[::-1], I32),
            pltpu.SMEM(near_count.shape, I32),
            pltpu.SMEM(far_cluster.shape, I32),
            vmem((3, 24, points.shape[1]), F32),
            vmem(bases.shape, F32),
            vmem(up_leaf.shape, F32),
            vmem(up_cluster.shape, F32),
            vmem(coupling_leaf.shape, F32),
            vmem(coupling_cluster.shape, F32),
            vmem(coupling_group.shape, F32),
            vmem(far_leaf.shape[::-1], I32),
            vmem(bases.shape, BF16),
            vmem(bases.shape, BF16),
            vmem((leaf_dev, far_two * rank, width), BF16),
            vmem((leaf_dev, far_two * rank, width), BF16),
            vmem((rank, rhs.shape[1]), BF16),
            vmem((rank, rhs.shape[1]), BF16),
            vmem((rank, n_grp * rank), BF16),
            vmem((rank, n_grp * rank), BF16),
            vmem((leaf_dev, width, 128), BF16),
            vmem((3 * leaf_dev, 128, width), BF16),
            vmem((3 * leaf_dev, 16, 2 * width), BF16),
            vmem((leaf_dev, nrhs, 128), F32),
            vmem((leaf_dev, nrhs, width), F32),
            vmem(rhs.shape, F32),
            vmem((nrhs, rank), F32),
            vmem((1, 128), I32),
            pltpu.SMEM((1, 128), I32),
            vmem((n_leaf, 128), I32),
            vmem((1, 128), I32),
            vmem((n_leaf, 128), I32),
            vmem((side, 8, 128), F32),
            vmem((side, side // 2, 8, 128), F32),
            vmem((side, 8, 128), F32),
            vmem((n_grp, 8, 128), F32),
            vmem((n_leaf - 1, 8, 128), F32),
            vmem((n_leaf - 1, 8, 128), F32),
            pltpu.SemaphoreType.DMA((12,)),
            pltpu.SemaphoreType.DMA,
            pltpu.SemaphoreType.DMA((2,)),
            pltpu.SemaphoreType.DMA((2,)),
            pltpu.SemaphoreType.DMA((6,)),
            pltpu.SemaphoreType.DMA((6,)),
        ],
        compiler_params=pltpu.CompilerParams(
            collective_id=0, has_side_effects=True, vmem_limit_bytes=32 * 1024 * 1024
        ),
    )(
        *(
            pltpu.with_memory_space_constraint(a, pltpu.HBM)
            for a in (
                near_list.T,
                near_count,
                far_cluster,
                points,
                rhs,
                bases,
                up_leaf,
                up_cluster,
                coupling_leaf,
                coupling_cluster,
                coupling_group,
                far_leaf.T,
            )
        )
    )


def solution(mesh):
    placed = (
        P(None, ("grp", "leaf")),
        P(None, ("grp", "leaf")),
        P(("grp", "leaf"), None, None),
        P(("grp", "leaf"), None, None),
        P(("grp", "leaf"), None, None),
        P(("grp", "leaf"), None, None, None),
        P(("grp", "leaf"), None, None, None),
        P("grp", None, None, None),
        P(("grp", "leaf"), None),
        P(("grp", "leaf")),
        P(("grp", "leaf"), None),
        P(("grp", "leaf"), None),
    )
    return jax.shard_map(
        per_device, mesh=mesh, in_specs=placed, out_specs=P(None, ("grp", "leaf")), check_vma=False
    )
```

```python
import functools

import jax
import jax.numpy as jnp
from jax import lax
from jax.experimental import pallas as pl
from jax.experimental.pallas import tpu as pltpu
from jax.sharding import PartitionSpec as P

F32, BF16, I32 = jnp.float32, jnp.bfloat16, jnp.int32
MESH = pl.DeviceIdType.MESH


def loop(start, stop, step, body):
    def some(i, c):
        for j in range(step):
            body(start + i * step + j)
        return c

    lax.fori_loop(0, (stop - start) // step, some, 0)


def iota(shape, dim):
    return lax.broadcasted_iota(I32, shape, dim)


def rounded(x):
    return x.astype(BF16).astype(F32)


def halves(x):
    high = x.astype(BF16)
    return high, (x - high.astype(F32)).astype(BF16)


def stack16(x):
    high = rounded(x)
    return jnp.concatenate([high, x - high], axis=0).astype(BF16)


def fold(x):
    return x[:8] + x[8:]


def nn(a, b):
    return lax.dot_general(a, b, (((1,), (0,)), ((), ())), preferred_element_type=F32)


def nt(a, b):
    return lax.dot_general(a, b, (((1,), (1,)), ((), ())), preferred_element_type=F32)


def split_dot(dot, x16, w):
    high, low = halves(w)
    return fold(dot(x16, high) + dot(x16, low))


def thirds(x):
    high = rounded(x)
    rest = x - high
    mid = rounded(rest)
    return high, mid, rest - mid


def norm_rows(norm, first):
    high, mid, low = thirds(norm)
    row = iota((32, norm.shape[1]), 0)
    at = row - first
    split = jnp.where(at == 0, high, jnp.where(at == 1, mid, jnp.where(at == 2, low, 0.0)))
    return jnp.where((row < 6) & ((at < 0) | (at > 2)), 1.0, split)


def kernel(
    side,
    n_grp,
    near_h,
    count_h,
    farc_h,
    pts_h,
    rhs_h,
    bases_h,
    upl_h,
    upc_h,
    cpl_h,
    cpc_h,
    cpg_h,
    farl_h,
    out_ref,
    near_s,
    count_s,
    farc_s,
    st,
    bases_v,
    upl_v,
    upc_v,
    cpl_v,
    cpc_v,
    cpg_v,
    farl_v,
    bhi,
    blo,
    vhi,
    vlo,
    whi,
    wlo,
    ghi,
    glo,
    left,
    right,
    weight,
    coef2,
    near_out,
    down,
    near_fc,
    tab_v,
    tab_s,
    ridx,
    ask,
    asked_by,
    ctz,
    cty,
    sums,
    gcb,
    rows_out,
    rows_in,
    load_sem,
    tab_sem,
    st_send,
    st_recv,
    x_send,
    x_recv,
):
    n_leaf = side * side
    many = n_grp * n_leaf
    leaf_dev = bases_v.shape[0]
    grp, leaf = lax.axis_index("grp"), lax.axis_index("leaf")
    y, z = lax.div(leaf, side), lax.rem(leaf, side)
    dev = grp * n_leaf + leaf

    def at_dev(d):
        return lax.div(d, n_leaf), lax.rem(d, n_leaf)

    after, before = at_dev(lax.rem(dev + 1, many)), at_dev(lax.rem(dev + many - 1, many))

    loads = {}
    plan = (
        ("farl", farl_h, farl_v),
        ("pts", pts_h, st.at[1, pl.ds(0, 16)]),
        ("rhs", rhs_h, st.at[1, pl.ds(16, 8)]),
        ("bases", bases_h, bases_v),
        ("upl", upl_h, upl_v),
        ("upc", upc_h, upc_v),
        ("cpl", cpl_h, cpl_v),
        ("cpc", cpc_h, cpc_v),
        ("cpg", cpg_h, cpg_v),
        ("near", near_h, near_s),
        ("count", count_h, count_s),
        ("farc", farc_h, farc_s),
    )
    for i, (name, src, dst) in enumerate(plan):
        loads[name] = pltpu.make_async_copy(src, dst, load_sem.at[i])
    first = ("rhs", "bases", "upl", "farl", "upc")
    for name in first:
        loads[name].start()


    barrier = pltpu.get_barrier_semaphore()

    def greet(who):
        pl.semaphore_signal(barrier, inc=1, device_id=who, device_id_type=MESH)

    greet(after)
    greet(before)

    loop(1, n_leaf, 7, lambda j: greet((grp, lax.rem(leaf + j, n_leaf))))
    loop(1, n_grp, 7, lambda j: greet((lax.rem(grp + j, n_grp), leaf)))

    for name, copy in loads.items():
        if name not in first:
            copy.start()

    def exchange(buf, at, peer, count, i):
        def go(j):
            pltpu.make_async_remote_copy(
                src_ref=buf.at[at],
                dst_ref=buf.at[at],
                send_sem=x_send.at[i],
                recv_sem=x_recv.at[i],
                device_id=peer(j),
                device_id_type=MESH,
            ).start()

        loop(1, count, 7, go)

    def arrived(ref, sem):
        pltpu.make_async_copy(ref, ref, sem).wait()

    def z_peer(j):
        return grp, y * side + lax.rem(z + j, side)

    def y_peer(j):
        return grp, lax.rem(y + j, side) * side + z

    def g_peer(j):
        return lax.rem(grp + j, n_grp), leaf

    loads["farl"].wait()
    far = farl_v[...]
    far_two = far.shape[0]
    asks = leaf_dev * far_two
    parts = [far[k : k + 1] for k in range(far_two)]
    row = jnp.concatenate([*parts, jnp.full((1, 128 - asks), -1, I32)], axis=1)
    ask[...] = row
    asked_by[pl.ds(leaf, 1)] = jnp.full((1, 128), -1, I32)
    owner = row >> 4
    lane_f, sub_f = iota((asks, 128), 1), iota((asks, 128), 0)
    spread = jnp.broadcast_to(owner.astype(F32), (asks, 128))
    column = jnp.sum(jnp.where(lane_f == sub_f, spread, 0.0), axis=1, keepdims=True)
    again = jnp.where((sub_f < lane_f) & (spread == column), 1.0, 0.0)
    again = jnp.max(again, axis=0, keepdims=True).astype(I32)
    place = ((leaf - (owner - grp * n_leaf)) & (n_leaf - 1)) - 1
    tab_v[...] = place * 2 + again
    tab_copy = pltpu.make_async_copy(tab_v, tab_s, tab_sem)
    tab_copy.start()

    loads["rhs"].wait()
    loads["bases"].wait()
    loads["upl"].wait()
    cc = jnp.zeros((16, 64), F32)
    for l in range(leaf_dev):
        x16 = stack16(st[1, 16:24, l * 128 : (l + 1) * 128])
        high, low = halves(bases_v[l])
        bhi[l], blo[l] = high, low
        two_high = jnp.concatenate([high, high], axis=0)
        two_low = jnp.concatenate([low, low], axis=0)
        c2 = fold(nt(x16, two_high) + nt(x16, two_low))
        coef2[l] = c2
        high, low = halves(upl_v[l])
        cc = cc + nn(stack16(c2), jnp.concatenate([high, low], axis=0))
    cc = fold(cc)
    loads["upc"].wait()
    term = split_dot(nn, stack16(cc), upc_v[0])
    ctz[z] = jnp.concatenate([cc, term], axis=1)

    loads["pts"].wait()
    pl.semaphore_wait(barrier, n_leaf + n_grp)

    def send_ask(j):
        pltpu.make_async_remote_copy(
            src_ref=ask,
            dst_ref=asked_by.at[pl.ds(leaf, 1)],
            send_sem=x_send.at[0],
            recv_sem=x_recv.at[0],
            device_id=(grp, lax.rem(leaf + j, n_leaf)),
            device_id_type=MESH,
        ).start()

    exchange(ctz, z, z_peer, side, 1)
    loop(1, n_leaf, 7, send_ask)
    def features(block, m):
        a = st[block, 0:16, pl.ds(pl.multiple_of(m * 128, 128), 128)]
        return a, 0.75 * jnp.sum(a * a, axis=0, keepdims=True)

    def put_right(block, m):
        b, norm = features(block, m)
        high, mid, low = thirds(b)
        parts = [high, mid, high, mid, low, high, norm_rows(norm, 0)]
        right[block * leaf_dev + m] = jnp.concatenate(parts, axis=0).T.astype(BF16)
        x = st[block, 16:24, pl.ds(pl.multiple_of(m * 128, 128), 128)]
        top = rounded(x)
        first = jnp.concatenate([top, x - top], axis=0)
        second = jnp.concatenate([top, jnp.zeros_like(top)], axis=0)
        weight[block * leaf_dev + m] = jnp.concatenate([first, second], axis=1).astype(BF16)

    def put_left(l):
        a, norm = features(1, l)
        high, mid, low = thirds(-1.5 * a)
        parts = [high, high, mid, mid, high, low, norm_rows(norm, 3)]
        left[l] = jnp.concatenate(parts, axis=0).astype(BF16)

    loop(0, leaf_dev, 4, put_left)
    loop(0, leaf_dev, 4, functools.partial(put_right, 1))
    sides = []
    for i, (who, slot) in enumerate(((after, 0), (before, 2))):
        copy = pltpu.make_async_remote_copy(
            src_ref=st.at[1],
            dst_ref=st.at[slot],
            send_sem=st_send.at[i],
            recv_sem=st_recv.at[i],
            device_id=who,
            device_id_type=MESH,
        )
        copy.start()
        sides.append(copy)


    loads["cpl"].wait()
    loads["cpg"].wait()

    def put_far(l):
        parts = [cpl_v[l, k] for k in range(far_two)]
        u = upl_v[l]
        parts += [u, jnp.zeros_like(u)]
        high, low = halves(jnp.concatenate(parts, axis=1))
        turned = jnp.concatenate([high, low], axis=0).T
        bh, bl = bhi[l], blo[l]
        both = nn(turned, jnp.concatenate([bh, bh], axis=0))
        both = both + nn(turned, jnp.concatenate([bl, bl], axis=0))
        high, low = halves(both)
        wide = far_two * 64
        vhi[l], vlo[l] = high[:wide], low[:wide]
        columns = pl.ds(pl.multiple_of(l * 128, 128), 128)
        whi[:, columns], wlo[:, columns] = high[wide : wide + 64], low[wide : wide + 64]

    loop(0, leaf_dev, 4, put_far)
    uc_high, uc_low = halves(upc_v[0])
    pieces = []
    for h in range(n_grp):
        high, low = halves(cpg_v[0, h])
        other = jnp.where(grp == h, 0.0, 1.0).astype(F32)
        pieces.append(other * (nn(uc_high, high) + nn(uc_high, low) + nn(uc_low, high)))
    ghi[...], glo[...] = halves(jnp.concatenate(pieces, axis=1))

    arrived(ctz.at[pl.ds(0, side - 1)], x_recv.at[1])
    low_lanes = iota((8, 128), 1) < 64
    total = ctz[0]
    for i in range(1, side):
        total = total + ctz[i]
    sums[y] = total
    exchange(sums, y, y_peer, side, 2)
    for i in range(side // 2):
        cty[y, i] = jnp.where(low_lanes, ctz[2 * i], pltpu.roll(ctz[2 * i + 1], 64, 1))
    exchange(cty, y, y_peer, side, 3)

    arrived(asked_by.at[pl.ds(0, n_leaf - 1)], x_recv.at[0])
    lane8 = iota((8, 128), 1)
    for i in range(n_leaf // 8):
        asked = asked_by[i * 8 : (i + 1) * 8]
        mine = (asked >> 4) == dev
        code = (lane8 * 16 + (asked & 15)).astype(F32)
        first = jnp.min(jnp.where(mine, code, 4096.0), axis=1, keepdims=True)
        last = jnp.max(jnp.where(mine, code, 0.0), axis=1, keepdims=True)
        ridx[i * 8 : (i + 1) * 8] = jnp.where(low_lanes, first, last).astype(I32) & 15

    def send_row(i):
        j = lax.rem(i * 27, n_leaf)
        who = lax.rem(leaf + j, n_leaf)
        index = jnp.broadcast_to(ridx[pl.ds(who, 1), :], (8, 128))
        picked = coef2[0]
        for l in range(1, leaf_dev):
            picked = jnp.where(index == l, coef2[l], picked)
        rows_out[j - 1] = picked
        pltpu.make_async_remote_copy(
            src_ref=rows_out.at[j - 1],
            dst_ref=rows_in.at[j - 1],
            send_sem=x_send.at[5],
            recv_sem=x_recv.at[5],
            device_id=(grp, who),
            device_id_type=MESH,
        ).start()

    loop(1, n_leaf, 7, send_row)
    arrived(sums.at[pl.ds(0, side - 1)], x_recv.at[2])
    total = sums[0]
    for i in range(1, side):
        total = total + sums[i]
    gcb[grp] = jnp.where(low_lanes, pltpu.roll(total, 64, 1), total)
    exchange(gcb, grp, g_peer, n_grp, 4)

    for copy, block in zip(sides, (0, 2)):
        copy.wait_recv()
        loop(0, leaf_dev, 4, functools.partial(put_right, block))
    loads["near"].wait()
    loads["count"].wait()
    slots = near_s.shape[0]
    base = (dev - 1) * leaf_dev

    def near_leaf(l):
        target = left[l]
        count = count_s[l]
        acc = jnp.zeros((16, 128), F32)
        for k in range(slots):
            m = jnp.clip(near_s[k, l] - base, 0, 3 * leaf_dev - 1)
            gap = jnp.maximum(nn(right[m], target), 1e-30)
            u = gap * lax.rsqrt(gap)
            value = (1.0 + u) * jnp.exp(-u)
            high = value.astype(BF16)
            low = (value - high.astype(F32)).astype(BF16)
            live = jnp.where(k < count, 1.0, 0.0).astype(F32)
            part = nn(weight[m], jnp.concatenate([high, low], axis=0))
            acc = acc + live * part
        near_out[l] = fold(acc)

    loop(0, leaf_dev, 4, near_leaf)

    arrived(cty.at[pl.ds(0, side - 1)], x_recv.at[3])
    loads["cpc"].wait()
    loads["farc"].wait()
    field_cluster = jnp.zeros((8, 64), F32)
    for k in range(cpc_v.shape[1]):
        f = jnp.clip(farc_s[0, k] - grp * n_leaf, 0, n_leaf - 1)
        fy, fz = lax.div(f, side), lax.rem(f, side)
        pair = cty[fy, lax.div(fz, 2)]
        flag = jnp.full((8, 128), lax.rem(fz, 2), I32)
        one = jnp.where(flag == 1, pltpu.roll(pair, 64, 1), pair)[:, :64]
        field_cluster = field_cluster + split_dot(nt, stack16(one), cpc_v[0, k])
    near_fc[...] = field_cluster

    arrived(gcb.at[pl.ds(0, n_grp - 1)], x_recv.at[4])
    chunks = [jnp.where(low_lanes, gcb[2 * i], gcb[2 * i + 1]) for i in range(n_grp // 2)]
    x16 = stack16(jnp.concatenate(chunks, axis=1))
    fc16 = stack16(fold(nt(x16, ghi[...]) + nt(x16, glo[...])) + near_fc[...])
    down[...] = fold(nn(fc16, whi[...]) + nn(fc16, wlo[...]))

    arrived(rows_in, x_recv.at[5])
    tab_copy.wait()
    for l in range(leaf_dev):
        chunks = []
        for pair in range(far_two // 2):
            both = []
            for half in range(2):
                t = tab_s[0, (2 * pair + half) * leaf_dev + l]
                got = rows_in[jnp.clip(t >> 1, 0, n_leaf - 2)]
                flag = jnp.full((8, 128), t & 1, I32)
                both.append(jnp.where(flag == half, got, pltpu.roll(got, 64, 1)))
            chunks.append(jnp.where(low_lanes, both[0], both[1]))
        x16 = stack16(jnp.concatenate(chunks, axis=1))
        part = fold(nn(x16, vhi[l]) + nn(x16, vlo[l]))
        columns = slice(l * 128, (l + 1) * 128)
        out_ref[:, columns] = part + (down[:, columns] + near_out[l])

    for copy in sides:
        copy.wait_send()
    for i, buf, n in ((1, ctz, side), (2, sums, side), (3, cty, side), (4, gcb, n_grp)):
        arrived(buf.at[pl.ds(0, n - 1)], x_send.at[i])
    arrived(asked_by.at[pl.ds(0, n_leaf - 1)], x_send.at[0])
    arrived(rows_out, x_send.at[5])


def per_device(
    points,
    rhs,
    bases,
    up_leaf,
    up_cluster,
    coupling_leaf,
    coupling_cluster,
    coupling_group,
    near_list,
    near_count,
    far_leaf,
    far_cluster,
):
    n_leaf, n_grp = lax.axis_size("leaf"), lax.axis_size("grp")
    side = round(n_leaf**0.5)
    leaf_dev, rank, width = bases.shape
    nrhs = rhs.shape[0]
    far_two = far_leaf.shape[1]
    anywhere = pl.BlockSpec(memory_space=pltpu.HBM)
    vmem = pltpu.VMEM
    return pl.pallas_call(
        functools.partial(kernel, side, n_grp),
        out_shape=vmem(rhs.shape, F32),
        in_specs=[anywhere] * 12,
        out_specs=pl.BlockSpec(memory_space=vmem),
        scratch_shapes=[
            pltpu.SMEM(near_list.shape[::-1], I32),
            pltpu.SMEM(near_count.shape, I32),
            pltpu.SMEM(far_cluster.shape, I32),
            vmem((3, 24, points.shape[1]), F32),
            vmem(bases.shape, F32),
            vmem(up_leaf.shape, F32),
            vmem(up_cluster.shape, F32),
            vmem(coupling_leaf.shape, F32),
            vmem(coupling_cluster.shape, F32),
            vmem(coupling_group.shape, F32),
            vmem(far_leaf.shape[::-1], I32),
            vmem(bases.shape, BF16),
            vmem(bases.shape, BF16),
            vmem((leaf_dev, far_two * rank, width), BF16),
            vmem((leaf_dev, far_two * rank, width), BF16),
            vmem((rank, rhs.shape[1]), BF16),
            vmem((rank, rhs.shape[1]), BF16),
            vmem((rank, n_grp * rank), BF16),
            vmem((rank, n_grp * rank), BF16),
            vmem((leaf_dev, width, 128), BF16),
            vmem((3 * leaf_dev, 128, width), BF16),
            vmem((3 * leaf_dev, 16, 2 * width), BF16),
            vmem((leaf_dev, nrhs, 128), F32),
            vmem((leaf_dev, nrhs, width), F32),
            vmem(rhs.shape, F32),
            vmem((nrhs, rank), F32),
            vmem((1, 128), I32),
            pltpu.SMEM((1, 128), I32),
            vmem((n_leaf, 128), I32),
            vmem((1, 128), I32),
            vmem((n_leaf, 128), I32),
            vmem((side, 8, 128), F32),
            vmem((side, side // 2, 8, 128), F32),
            vmem((side, 8, 128), F32),
            vmem((n_grp, 8, 128), F32),
            vmem((n_leaf - 1, 8, 128), F32),
            vmem((n_leaf - 1, 8, 128), F32),
            pltpu.SemaphoreType.DMA((12,)),
            pltpu.SemaphoreType.DMA,
            pltpu.SemaphoreType.DMA((2,)),
            pltpu.SemaphoreType.DMA((2,)),
            pltpu.SemaphoreType.DMA((6,)),
            pltpu.SemaphoreType.DMA((6,)),
        ],
        compiler_params=pltpu.CompilerParams(
            collective_id=0, has_side_effects=True, vmem_limit_bytes=32 * 1024 * 1024
        ),
    )(
        *(
            pltpu.with_memory_space_constraint(a, pltpu.HBM)
            for a in (
                near_list.T,
                near_count,
                far_cluster,
                points,
                rhs,
                bases,
                up_leaf,
                up_cluster,
                coupling_leaf,
                coupling_cluster,
                coupling_group,
                far_leaf.T,
            )
        )
    )


def solution(mesh):
    placed = (
        P(None, ("grp", "leaf")),
        P(None, ("grp", "leaf")),
        P(("grp", "leaf"), None, None),
        P(("grp", "leaf"), None, None),
        P(("grp", "leaf"), None, None),
        P(("grp", "leaf"), None, None, None),
        P(("grp", "leaf"), None, None, None),
        P("grp", None, None, None),
        P(("grp", "leaf"), None),
        P(("grp", "leaf")),
        P(("grp", "leaf"), None),
        P(("grp", "leaf"), None),
    )
    return jax.shard_map(
        per_device, mesh=mesh, in_specs=placed, out_specs=P(None, ("grp", "leaf")), check_vma=False
    )
```

```python
import functools

import jax
import jax.numpy as jnp
from jax import lax
from jax.experimental import pallas as pl
from jax.experimental.pallas import tpu as pltpu
from jax.sharding import PartitionSpec as P

F32, BF16, I32 = jnp.float32, jnp.bfloat16, jnp.int32
MESH = pl.DeviceIdType.MESH


def loop(start, stop, step, body):
    def some(i, c):
        for j in range(step):
            body(start + i * step + j)
        return c

    lax.fori_loop(0, (stop - start) // step, some, 0)


def iota(shape, dim):
    return lax.broadcasted_iota(I32, shape, dim)


def rounded(x):
    return x.astype(BF16).astype(F32)


def halves(x):
    high = x.astype(BF16)
    return high, (x - high.astype(F32)).astype(BF16)


def stack16(x):
    high = rounded(x)
    return jnp.concatenate([high, x - high], axis=0).astype(BF16)


def fold(x):
    return x[:8] + x[8:]


def nn(a, b):
    return lax.dot_general(a, b, (((1,), (0,)), ((), ())), preferred_element_type=F32)


def nt(a, b):
    return lax.dot_general(a, b, (((1,), (1,)), ((), ())), preferred_element_type=F32)


def split_dot(dot, x16, w):
    high, low = halves(w)
    return fold(dot(x16, high) + dot(x16, low))


def thirds(x):
    high = rounded(x)
    rest = x - high
    mid = rounded(rest)
    return high, mid, rest - mid


def norm_rows(norm, first):
    high, mid, low = thirds(norm)
    row = iota((32, norm.shape[1]), 0)
    at = row - first
    split = jnp.where(at == 0, high, jnp.where(at == 1, mid, jnp.where(at == 2, low, 0.0)))
    return jnp.where((row < 6) & ((at < 0) | (at > 2)), 1.0, split)


def kernel(
    side,
    n_grp,
    near_h,
    count_h,
    farc_h,
    pts_h,
    rhs_h,
    bases_h,
    upl_h,
    upc_h,
    cpl_h,
    cpc_h,
    cpg_h,
    farl_h,
    out_ref,
    near_s,
    count_s,
    farc_s,
    st,
    bases_v,
    upl_v,
    upc_v,
    cpl_v,
    cpc_v,
    cpg_v,
    farl_v,
    bhi,
    blo,
    vhi,
    vlo,
    whi,
    wlo,
    ghi,
    glo,
    left,
    right,
    weight,
    coef2,
    near_out,
    down,
    near_fc,
    tab_v,
    tab_s,
    ridx,
    ask,
    asked_by,
    ctz,
    cty,
    sums,
    gcb,
    rows_out,
    rows_in,
    load_sem,
    tab_sem,
    st_send,
    st_recv,
    x_send,
    x_recv,
):
    n_leaf = side * side
    many = n_grp * n_leaf
    leaf_dev = bases_v.shape[0]
    grp, leaf = lax.axis_index("grp"), lax.axis_index("leaf")
    y, z = lax.div(leaf, side), lax.rem(leaf, side)
    dev = grp * n_leaf + leaf

    def at_dev(d):
        return lax.div(d, n_leaf), lax.rem(d, n_leaf)

    after, before = at_dev(lax.rem(dev + 1, many)), at_dev(lax.rem(dev + many - 1, many))

    loads = {}
    plan = (
        ("farl", farl_h, farl_v),
        ("pts", pts_h, st.at[1, pl.ds(0, 16)]),
        ("rhs", rhs_h, st.at[1, pl.ds(16, 8)]),
        ("bases", bases_h, bases_v),
        ("upl", upl_h, upl_v),
        ("upc", upc_h, upc_v),
        ("cpl", cpl_h, cpl_v),
        ("cpc", cpc_h, cpc_v),
        ("cpg", cpg_h, cpg_v),
        ("near", near_h, near_s),
        ("count", count_h, count_s),
        ("farc", farc_h, farc_s),
    )
    for i, (name, src, dst) in enumerate(plan):
        loads[name] = pltpu.make_async_copy(src, dst, load_sem.at[i])
    first = ("rhs", "bases", "upl", "farl", "upc")
    for name in first:
        loads[name].start()


    barrier = pltpu.get_barrier_semaphore()

    def greet(who):
        pl.semaphore_signal(barrier, inc=1, device_id=who, device_id_type=MESH)

    greet(after)
    greet(before)

    loop(1, n_leaf, 7, lambda j: greet((grp, lax.rem(leaf + j * 27, n_leaf))))
    loop(1, n_grp, 7, lambda j: greet((lax.rem(grp + j, n_grp), leaf)))

    for name, copy in loads.items():
        if name not in first:
            copy.start()

    def exchange(buf, at, peer, count, i):
        def go(j):
            pltpu.make_async_remote_copy(
                src_ref=buf.at[at],
                dst_ref=buf.at[at],
                send_sem=x_send.at[i],
                recv_sem=x_recv.at[i],
                device_id=peer(j),
                device_id_type=MESH,
            ).start()

        loop(1, count, 7, go)

    def arrived(ref, sem):
        pltpu.make_async_copy(ref, ref, sem).wait()

    def z_peer(j):
        return grp, y * side + lax.rem(z + j, side)

    def y_peer(j):
        return grp, lax.rem(y + j, side) * side + z

    def g_peer(j):
        return lax.rem(grp + j, n_grp), leaf

    loads["farl"].wait()
    far = farl_v[...]
    far_two = far.shape[0]
    asks = leaf_dev * far_two
    parts = [far[k : k + 1] for k in range(far_two)]
    row = jnp.concatenate([*parts, jnp.full((1, 128 - asks), -1, I32)], axis=1)
    ask[...] = row
    asked_by[pl.ds(leaf, 1)] = jnp.full((1, 128), -1, I32)
    owner = row >> 4
    lane_f, sub_f = iota((asks, 128), 1), iota((asks, 128), 0)
    spread = jnp.broadcast_to(owner.astype(F32), (asks, 128))
    column = jnp.sum(jnp.where(lane_f == sub_f, spread, 0.0), axis=1, keepdims=True)
    again = jnp.where((sub_f < lane_f) & (spread == column), 1.0, 0.0)
    again = jnp.max(again, axis=0, keepdims=True).astype(I32)
    place = ((leaf - (owner - grp * n_leaf)) & (n_leaf - 1)) - 1
    tab_v[...] = place * 2 + again
    tab_copy = pltpu.make_async_copy(tab_v, tab_s, tab_sem)
    tab_copy.start()

    loads["rhs"].wait()
    loads["bases"].wait()
    loads["upl"].wait()
    cc = jnp.zeros((16, 64), F32)
    for l in range(leaf_dev):
        x16 = stack16(st[1, 16:24, l * 128 : (l + 1) * 128])
        high, low = halves(bases_v[l])
        bhi[l], blo[l] = high, low
        two_high = jnp.concatenate([high, high], axis=0)
        two_low = jnp.concatenate([low, low], axis=0)
        c2 = fold(nt(x16, two_high) + nt(x16, two_low))
        coef2[l] = c2
        high, low = halves(upl_v[l])
        cc = cc + nn(stack16(c2), jnp.concatenate([high, low], axis=0))
    cc = fold(cc)
    loads["upc"].wait()
    term = split_dot(nn, stack16(cc), upc_v[0])
    ctz[z] = jnp.concatenate([cc, term], axis=1)

    loads["pts"].wait()
    pl.semaphore_wait(barrier, n_leaf + n_grp)

    def send_ask(j):
        pltpu.make_async_remote_copy(
            src_ref=ask,
            dst_ref=asked_by.at[pl.ds(leaf, 1)],
            send_sem=x_send.at[0],
            recv_sem=x_recv.at[0],
            device_id=(grp, lax.rem(leaf + j * 27, n_leaf)),
            device_id_type=MESH,
        ).start()

    exchange(ctz, z, z_peer, side, 1)
    loop(1, n_leaf, 7, send_ask)
    def features(block, m):
        a = st[block, 0:16, pl.ds(pl.multiple_of(m * 128, 128), 128)]
        return a, 0.75 * jnp.sum(a * a, axis=0, keepdims=True)

    def put_right(block, m):
        b, norm = features(block, m)
        high, mid, low = thirds(b)
        parts = [high, mid, high, mid, low, high, norm_rows(norm, 0)]
        right[block * leaf_dev + m] = jnp.concatenate(parts, axis=0).T.astype(BF16)
        x = st[block, 16:24, pl.ds(pl.multiple_of(m * 128, 128), 128)]
        top = rounded(x)
        first = jnp.concatenate([top, x - top], axis=0)
        second = jnp.concatenate([top, jnp.zeros_like(top)], axis=0)
        weight[block * leaf_dev + m] = jnp.concatenate([first, second], axis=1).astype(BF16)

    def put_left(l):
        a, norm = features(1, l)
        high, mid, low = thirds(-1.5 * a)
        parts = [high, high, mid, mid, high, low, norm_rows(norm, 3)]
        left[l] = jnp.concatenate(parts, axis=0).astype(BF16)

    loop(0, leaf_dev, 4, put_left)
    loop(0, leaf_dev, 4, functools.partial(put_right, 1))
    sides = []
    for i, (who, slot) in enumerate(((after, 0), (before, 2))):
        copy = pltpu.make_async_remote_copy(
            src_ref=st.at[1],
            dst_ref=st.at[slot],
            send_sem=st_send.at[i],
            recv_sem=st_recv.at[i],
            device_id=who,
            device_id_type=MESH,
        )
        copy.start()
        sides.append(copy)


    loads["cpl"].wait()
    loads["cpg"].wait()

    def put_far(l):
        parts = [cpl_v[l, k] for k in range(far_two)]
        u = upl_v[l]
        parts += [u, jnp.zeros_like(u)]
        high, low = halves(jnp.concatenate(parts, axis=1))
        turned = jnp.concatenate([high, low], axis=0).T
        bh, bl = bhi[l], blo[l]
        both = nn(turned, jnp.concatenate([bh, bh], axis=0))
        both = both + nn(turned, jnp.concatenate([bl, bl], axis=0))
        high, low = halves(both)
        wide = far_two * 64
        vhi[l], vlo[l] = high[:wide], low[:wide]
        columns = pl.ds(pl.multiple_of(l * 128, 128), 128)
        whi[:, columns], wlo[:, columns] = high[wide : wide + 64], low[wide : wide + 64]

    loop(0, leaf_dev, 4, put_far)
    uc_high, uc_low = halves(upc_v[0])
    pieces = []
    for h in range(n_grp):
        high, low = halves(cpg_v[0, h])
        other = jnp.where(grp == h, 0.0, 1.0).astype(F32)
        pieces.append(other * (nn(uc_high, high) + nn(uc_high, low) + nn(uc_low, high)))
    ghi[...], glo[...] = halves(jnp.concatenate(pieces, axis=1))

    arrived(ctz.at[pl.ds(0, side - 1)], x_recv.at[1])
    low_lanes = iota((8, 128), 1) < 64
    total = ctz[0]
    for i in range(1, side):
        total = total + ctz[i]
    sums[y] = total
    exchange(sums, y, y_peer, side, 2)
    for i in range(side // 2):
        cty[y, i] = jnp.where(low_lanes, ctz[2 * i], pltpu.roll(ctz[2 * i + 1], 64, 1))
    exchange(cty, y, y_peer, side, 3)

    arrived(asked_by.at[pl.ds(0, n_leaf - 1)], x_recv.at[0])
    lane8 = iota((8, 128), 1)
    for i in range(n_leaf // 8):
        asked = asked_by[i * 8 : (i + 1) * 8]
        mine = (asked >> 4) == dev
        code = (lane8 * 16 + (asked & 15)).astype(F32)
        first = jnp.min(jnp.where(mine, code, 4096.0), axis=1, keepdims=True)
        last = jnp.max(jnp.where(mine, code, 0.0), axis=1, keepdims=True)
        ridx[i * 8 : (i + 1) * 8] = jnp.where(low_lanes, first, last).astype(I32) & 15

    def send_row(i):
        j = lax.rem(i * 27, n_leaf)
        who = lax.rem(leaf + j, n_leaf)
        index = jnp.broadcast_to(ridx[pl.ds(who, 1), :], (8, 128))
        picked = coef2[0]
        for l in range(1, leaf_dev):
            picked = jnp.where(index == l, coef2[l], picked)
        rows_out[j - 1] = picked
        pltpu.make_async_remote_copy(
            src_ref=rows_out.at[j - 1],
            dst_ref=rows_in.at[j - 1],
            send_sem=x_send.at[5],
            recv_sem=x_recv.at[5],
            device_id=(grp, who),
            device_id_type=MESH,
        ).start()

    loop(1, n_leaf, 7, send_row)
    arrived(sums.at[pl.ds(0, side - 1)], x_recv.at[2])
    total = sums[0]
    for i in range(1, side):
        total = total + sums[i]
    gcb[grp] = jnp.where(low_lanes, pltpu.roll(total, 64, 1), total)
    exchange(gcb, grp, g_peer, n_grp, 4)

    for copy, block in zip(sides, (0, 2)):
        copy.wait_recv()
        loop(0, leaf_dev, 4, functools.partial(put_right, block))
    loads["near"].wait()
    loads["count"].wait()
    slots = near_s.shape[0]
    base = (dev - 1) * leaf_dev

    def near_leaf(l):
        target = left[l]
        count = count_s[l]
        acc = jnp.zeros((16, 128), F32)
        for k in range(slots):
            m = jnp.clip(near_s[k, l] - base, 0, 3 * leaf_dev - 1)
            gap = jnp.maximum(nn(right[m], target), 1e-30)
            u = gap * lax.rsqrt(gap)
            value = (1.0 + u) * jnp.exp(-u)
            high = value.astype(BF16)
            low = (value - high.astype(F32)).astype(BF16)
            live = jnp.where(k < count, 1.0, 0.0).astype(F32)
            part = nn(weight[m], jnp.concatenate([high, low], axis=0))
            acc = acc + live * part
        near_out[l] = fold(acc)

    loop(0, leaf_dev, 4, near_leaf)

    arrived(cty.at[pl.ds(0, side - 1)], x_recv.at[3])
    loads["cpc"].wait()
    loads["farc"].wait()
    field_cluster = jnp.zeros((8, 64), F32)
    for k in range(cpc_v.shape[1]):
        f = jnp.clip(farc_s[0, k] - grp * n_leaf, 0, n_leaf - 1)
        fy, fz = lax.div(f, side), lax.rem(f, side)
        pair = cty[fy, lax.div(fz, 2)]
        flag = jnp.full((8, 128), lax.rem(fz, 2), I32)
        one = jnp.where(flag == 1, pltpu.roll(pair, 64, 1), pair)[:, :64]
        field_cluster = field_cluster + split_dot(nt, stack16(one), cpc_v[0, k])
    near_fc[...] = field_cluster

    arrived(gcb.at[pl.ds(0, n_grp - 1)], x_recv.at[4])
    chunks = [jnp.where(low_lanes, gcb[2 * i], gcb[2 * i + 1]) for i in range(n_grp // 2)]
    x16 = stack16(jnp.concatenate(chunks, axis=1))
    fc16 = stack16(fold(nt(x16, ghi[...]) + nt(x16, glo[...])) + near_fc[...])
    down[...] = fold(nn(fc16, whi[...]) + nn(fc16, wlo[...]))

    arrived(rows_in, x_recv.at[5])
    tab_copy.wait()
    for l in range(leaf_dev):
        chunks = []
        for pair in range(far_two // 2):
            both = []
            for half in range(2):
                t = tab_s[0, (2 * pair + half) * leaf_dev + l]
                got = rows_in[jnp.clip(t >> 1, 0, n_leaf - 2)]
                flag = jnp.full((8, 128), t & 1, I32)
                both.append(jnp.where(flag == half, got, pltpu.roll(got, 64, 1)))
            chunks.append(jnp.where(low_lanes, both[0], both[1]))
        x16 = stack16(jnp.concatenate(chunks, axis=1))
        part = fold(nn(x16, vhi[l]) + nn(x16, vlo[l]))
        columns = slice(l * 128, (l + 1) * 128)
        out_ref[:, columns] = part + (down[:, columns] + near_out[l])

    for copy in sides:
        copy.wait_send()
    for i, buf, n in ((1, ctz, side), (2, sums, side), (3, cty, side), (4, gcb, n_grp)):
        arrived(buf.at[pl.ds(0, n - 1)], x_send.at[i])
    arrived(asked_by.at[pl.ds(0, n_leaf - 1)], x_send.at[0])
    arrived(rows_out, x_send.at[5])


def per_device(
    points,
    rhs,
    bases,
    up_leaf,
    up_cluster,
    coupling_leaf,
    coupling_cluster,
    coupling_group,
    near_list,
    near_count,
    far_leaf,
    far_cluster,
):
    n_leaf, n_grp = lax.axis_size("leaf"), lax.axis_size("grp")
    side = round(n_leaf**0.5)
    leaf_dev, rank, width = bases.shape
    nrhs = rhs.shape[0]
    far_two = far_leaf.shape[1]
    anywhere = pl.BlockSpec(memory_space=pltpu.HBM)
    vmem = pltpu.VMEM
    return pl.pallas_call(
        functools.partial(kernel, side, n_grp),
        out_shape=vmem(rhs.shape, F32),
        in_specs=[anywhere] * 12,
        out_specs=pl.BlockSpec(memory_space=vmem),
        scratch_shapes=[
            pltpu.SMEM(near_list.shape[::-1], I32),
            pltpu.SMEM(near_count.shape, I32),
            pltpu.SMEM(far_cluster.shape, I32),
            vmem((3, 24, points.shape[1]), F32),
            vmem(bases.shape, F32),
            vmem(up_leaf.shape, F32),
            vmem(up_cluster.shape, F32),
            vmem(coupling_leaf.shape, F32),
            vmem(coupling_cluster.shape, F32),
            vmem(coupling_group.shape, F32),
            vmem(far_leaf.shape[::-1], I32),
            vmem(bases.shape, BF16),
            vmem(bases.shape, BF16),
            vmem((leaf_dev, far_two * rank, width), BF16),
            vmem((leaf_dev, far_two * rank, width), BF16),
            vmem((rank, rhs.shape[1]), BF16),
            vmem((rank, rhs.shape[1]), BF16),
            vmem((rank, n_grp * rank), BF16),
            vmem((rank, n_grp * rank), BF16),
            vmem((leaf_dev, width, 128), BF16),
            vmem((3 * leaf_dev, 128, width), BF16),
            vmem((3 * leaf_dev, 16, 2 * width), BF16),
            vmem((leaf_dev, nrhs, 128), F32),
            vmem((leaf_dev, nrhs, width), F32),
            vmem(rhs.shape, F32),
            vmem((nrhs, rank), F32),
            vmem((1, 128), I32),
            pltpu.SMEM((1, 128), I32),
            vmem((n_leaf, 128), I32),
            vmem((1, 128), I32),
            vmem((n_leaf, 128), I32),
            vmem((side, 8, 128), F32),
            vmem((side, side // 2, 8, 128), F32),
            vmem((side, 8, 128), F32),
            vmem((n_grp, 8, 128), F32),
            vmem((n_leaf - 1, 8, 128), F32),
            vmem((n_leaf - 1, 8, 128), F32),
            pltpu.SemaphoreType.DMA((12,)),
            pltpu.SemaphoreType.DMA,
            pltpu.SemaphoreType.DMA((2,)),
            pltpu.SemaphoreType.DMA((2,)),
            pltpu.SemaphoreType.DMA((6,)),
            pltpu.SemaphoreType.DMA((6,)),
        ],
        compiler_params=pltpu.CompilerParams(
            collective_id=0, has_side_effects=True, vmem_limit_bytes=32 * 1024 * 1024
        ),
    )(
        *(
            pltpu.with_memory_space_constraint(a, pltpu.HBM)
            for a in (
                near_list.T,
                near_count,
                far_cluster,
                points,
                rhs,
                bases,
                up_leaf,
                up_cluster,
                coupling_leaf,
                coupling_cluster,
                coupling_group,
                far_leaf.T,
            )
        )
    )


def solution(mesh):
    placed = (
        P(None, ("grp", "leaf")),
        P(None, ("grp", "leaf")),
        P(("grp", "leaf"), None, None),
        P(("grp", "leaf"), None, None),
        P(("grp", "leaf"), None, None),
        P(("grp", "leaf"), None, None, None),
        P(("grp", "leaf"), None, None, None),
        P("grp", None, None, None),
        P(("grp", "leaf"), None),
        P(("grp", "leaf")),
        P(("grp", "leaf"), None),
        P(("grp", "leaf"), None),
    )
    return jax.shard_map(
        per_device, mesh=mesh, in_specs=placed, out_specs=P(None, ("grp", "leaf")), check_vma=False
    )
```
